32 devices in a mesh: groups: 2 (over y), frames: 8 (over z, x), bins: 2 (over core).
Axes of the slice: x: 2, y: 2, z: 4, core: 2. Of those that a mesh axis runs over, the one named last changes fastest.
Arguments:
- spectrum: float32 [2048, 32768], P('bins', ('groups', 'frames')), parts along dimension 1, may hold values from 0.1 to 10
- atoms_by_bin: float32 [256, 4096], P('frames', ('groups', 'bins')), parts along dimension 1, may hold values from 0.03 to 2.12, as said below
- activations: float32 [256, 32768], P('bins', ('groups', 'frames')), parts along dimension 1, may hold values from 0.01 to 2.05, as said below
Outputs:
- new_activations: float32 [256, 32768], P('bins', ('groups', 'frames')), parts along dimension 1
- new_atoms: float32 [256, 4096], P('frames', ('groups', 'bins')), parts along dimension 1
The draws below stay inside these ranges and needn't reach their ends.
There are 2 independent parts, one for each index of `groups`. The reference program is written for one: setup_inputs(seed, part) draws one part's arguments, and reference() takes and returns one part's arrays. A program takes and returns all parts, laid end to end along the dimension named above; each array names one. Nothing has to cross between parts.
Inputs may be any that keep to these rules, and one draw needn't show every extreme that they name: `atoms_by_bin`: every entry is positive. `activations`: every entry is positive.
All inputs are finite; a program needn't handle non-finite values.
Results may differ from the reference program's by a relative error of at most 0.0003.
Values sent between devices are 32-bit elements; how exact they have to be, the bound alone decides.
No kernel may reach another device: no remote copies, remote signals or barrier semaphores. Data moves between devices by JAX's collectives and lax.ppermute only.
A program may use at most 64 MiB of HBM per device.

```python
import math
import jax
import jax.numpy as jnp
from jax import lax

F = 2048
K = 256
FR_DEV = 2048
N = 16384


def draw_atoms_by_bin(key, part):
    key = jax.random.fold_in(key, 11)
    key_center, key_width, key_rough, key_floor = jax.random.split(key, 4)
    centers = jax.random.uniform(key_center, (K, 1), jnp.float32, 0.0, 1.0) * F
    widths = F * jnp.exp(jax.random.uniform(key_width, (K, 1), jnp.float32, math.log(1.0 / 64.0), math.log(1.0 / 16.0)))
    position = jnp.arange(F, dtype=jnp.float32)[None, :]
    band = jnp.exp(-0.5 * ((position - centers) / widths) ** 2)
    rough = jnp.exp(jax.random.uniform(key_rough, (K, F), jnp.float32, math.log(0.5), math.log(2.0)))
    background = jnp.exp(jax.random.uniform(key_floor, (K, F), jnp.float32, math.log(0.03), math.log(0.12)))
    return (background + band * rough).astype(jnp.float32)


def draw_activations(key, part):
    key = jax.random.fold_in(key, 23)
    key_base, key_mask, key_active = jax.random.split(key, 3)
    base = jnp.exp(jax.random.uniform(key_base, (K, N), jnp.float32, math.log(0.01), math.log(0.05)))
    active = jnp.exp(jax.random.uniform(key_active, (K, N), jnp.float32, math.log(0.5), math.log(2.0)))
    chosen = jax.random.bernoulli(key_mask, 8.0 / K, (K, N))
    return (base + jnp.where(chosen, active, 0.0)).astype(jnp.float32)


def steps_of(stream_key, extent, shards, smallest, top_value):
    factor_of, own = 1.0, jax.random.fold_in(stream_key, 6)
    for axis_at, parts in shards:
        draws = jnp.exp(jax.random.uniform(jax.random.fold_in(own, axis_at), (parts,), jnp.float32, smallest / len(shards), top_value / len(shards)))
        factor_of = factor_of * jnp.repeat(draws, extent[axis_at] // parts).reshape([-1 if axis == axis_at else 1 for axis in range(len(extent))])
    return factor_of


def setup_inputs(seed: int = 0, part: int = 0) -> dict:
    key_of = jax.random.split(jax.random.key(seed), 4)
    part_splits = jax.random.split(jax.random.fold_in(key_of[3], part), 4)
    spectrum = jnp.clip(jnp.exp(math.log(10.0) - 4.6051702 * jax.random.uniform(part_splits[0], (F, N), jnp.float32) ** steps_of(part_splits[0], (F, N), ((0, 2), (1, 8)), -0.2, 0.2)), 0.1, 10.0)
    atoms_by_bin = draw_atoms_by_bin(jax.random.fold_in(jax.random.fold_in(key_of[3], part), 71), part)
    activations = draw_activations(jax.random.fold_in(jax.random.fold_in(key_of[3], part), 71), part)
    return dict(spectrum=spectrum, atoms_by_bin=atoms_by_bin, activations=activations)


def reference(spectrum, atoms_by_bin, activations):
    highest = lax.Precision.HIGHEST
    column_mass = jnp.sum(atoms_by_bin, axis=1)
    blocks = N // FR_DEV

    def advance(carry, index):
        numer, row_mass = carry
        start = (index * FR_DEV).astype(jnp.int32)
        values = lax.dynamic_slice_in_dim(spectrum, start, FR_DEV, 1)
        old = lax.dynamic_slice_in_dim(activations, start, FR_DEV, 1)
        model = jnp.dot(atoms_by_bin.T, old, precision=highest, preferred_element_type=jnp.float32)
        ratio = values / model
        fresh = old * jnp.dot(atoms_by_bin, ratio, precision=highest, preferred_element_type=jnp.float32) / column_mass[:, None]
        model_next = jnp.dot(atoms_by_bin.T, fresh, precision=highest, preferred_element_type=jnp.float32)
        ratio_next = values / model_next
        numer = numer + jnp.dot(fresh, ratio_next.T, precision=highest, preferred_element_type=jnp.float32)
        row_mass = row_mass + jnp.sum(fresh, axis=1)
        return (numer, row_mass), fresh

    start_carry = (jnp.zeros((K, F), jnp.float32), jnp.zeros((K,), jnp.float32))
    (numer, row_mass), pieces = lax.scan(advance, start_carry, jnp.arange(blocks, dtype=jnp.int32))
    new_activations = jnp.transpose(pieces, (1, 0, 2)).reshape(K, N)
    new_atoms = atoms_by_bin * numer / row_mass[:, None]
    return new_activations, new_atoms
```

```python
import functools

import jax
import jax.numpy as jnp
from jax import lax
from jax.experimental import pallas as pl
from jax.experimental.pallas import tpu as pltpu
from jax.sharding import PartitionSpec as P

f32, bf16 = jnp.float32, jnp.bfloat16
VMEM_LIMIT = 40 * 2**20


def split(x):
    hi = x.astype(bf16)
    return hi, (x - hi.astype(f32)).astype(bf16)


def dot(a, b):
    return jnp.dot(a, b, preferred_element_type=f32)


def dot_nt(a, b):
    return lax.dot_general(a, b, (((1,), (1,)), ((), ())), preferred_element_type=f32)


def quotient(v, m):
    r = pl.reciprocal(m, approx=True)
    r = r * (2.0 - m * r)
    return v * r


def rows_at(start, rows):
    return pl.ds(pl.multiple_of(start * rows, rows), rows)


def first_kernel(idx, v, hown, hoth, *rest, n_w, n_dev, fc):
    ws = rest[:n_w]
    numer, wt3o, mass = rest[n_w : n_w + 3]
    w2, wt3, h, rhi, rlo = rest[n_w + 3 :]
    bins = v.shape[0]
    atoms = h.shape[0]

    @pl.when(pl.program_id(0) == 0)
    def _():
        rows = ws[0].shape[0]
        for s, w in enumerate(ws):
            x = w[...]
            hi, lo = split(x)
            src = lax.rem(idx[0] - s + n_dev, n_dev) if n_w > 1 else 0
            at = rows_at(src, rows)
            at2 = rows_at(src + atoms // rows, rows)
            w2[at, :] = hi
            w2[at2, :] = lo
            mass[at, :] = jnp.broadcast_to(jnp.sum(x, axis=1, keepdims=True), (rows, 128))
        t = w2[:atoms, :].T
        wt3[:, :atoms] = t
        wt3[:, 2 * atoms :] = t
        wt3[:, atoms : 2 * atoms] = w2[atoms:, :].T
        wt3o[...] = wt3[...]

    half = hown.shape[0]
    h[rows_at(idx[1], half), :] = hown[...]
    h[rows_at(1 - idx[1], half), :] = hoth[...]
    hhi, hlo = split(h[...])
    h3 = jnp.concatenate([hhi, hhi, hlo], axis=0)
    for f in range(0, bins, fc):
        m = dot(wt3[f : f + fc, :], h3)
        hi, lo = split(quotient(v[f : f + fc, :], m))
        rhi[f : f + fc, :] = hi
        rlo[f : f + fc, :] = lo
    numer[...] = dot(w2[:atoms, :], rhi[...]) + dot(w2[atoms:, :], rhi[...]) + dot(w2[:atoms, :], rlo[...])


def call_first(idx, spectrum, hown, hoth, ws, n_dev, block=1024, fc=256):
    bins, frames = spectrum.shape
    half = hown.shape[0]
    atoms = 2 * half
    block = min(block, frames)
    part = lambda r: pl.BlockSpec((r, block), lambda i: (0, i))
    whole = lambda a: pl.BlockSpec(a, lambda i: (0, 0))
    return pl.pallas_call(
        functools.partial(first_kernel, n_w=len(ws), n_dev=n_dev, fc=fc),
        grid=(frames // block,),
        in_specs=[pl.BlockSpec(memory_space=pltpu.SMEM), part(bins), part(half), part(half)]
        + [whole(w.shape) for w in ws],
        out_specs=[part(atoms), whole((bins, 3 * atoms)), whole((atoms, 128))],
        out_shape=[
            jax.ShapeDtypeStruct((atoms, frames), f32),
            jax.ShapeDtypeStruct((bins, 3 * atoms), bf16),
            jax.ShapeDtypeStruct((atoms, 128), f32),
        ],
        scratch_shapes=[
            pltpu.VMEM((2 * atoms, bins), bf16),
            pltpu.VMEM((bins, 3 * atoms), bf16),
            pltpu.VMEM((atoms, block), f32),
            pltpu.VMEM((bins, block), bf16),
            pltpu.VMEM((bins, block), bf16),
        ],
        compiler_params=pltpu.CompilerParams(vmem_limit_bytes=VMEM_LIMIT),
    )(idx, spectrum, hown, hoth, *ws)


def second_kernel(idx, v, hown, hoth, nown, noth, massa, massb, wt3, *rest, n_out, n_dev, fc, steps):
    newact = rest[0]
    outs = rest[1 : 1 + n_out]
    h, acc, row_acc, accn = rest[1 + n_out :]
    bins = v.shape[0]
    atoms = h.shape[0]
    half = hown.shape[0]
    i = pl.program_id(0)
    own = rows_at(idx[1], half)
    oth = rows_at(1 - idx[1], half)

    def fresh_of(old, at):
        mass = massa[at, :] + massb[at, :]
        return old[...] * (nown[at, :] + noth[at, :]) / mass[:, :1]

    fresh_own = fresh_of(hown, own)
    newact[...] = fresh_own
    h[own, :] = fresh_own
    h[oth, :] = fresh_of(hoth, oth)
    fresh = h[...]
    hhi, hlo = split(fresh)
    h3 = jnp.concatenate([hhi, hhi, hlo], axis=0)

    @pl.when(i == 0)
    def _():
        row_acc[...] = jnp.zeros_like(row_acc)
        acc[...] = jnp.zeros_like(acc)

    row_acc[...] += jnp.broadcast_to(jnp.sum(fresh, axis=1, keepdims=True), row_acc.shape)
    for f in range(0, bins, fc):
        m = dot(wt3[f : f + fc, :], h3)
        hi, lo = split(quotient(v[f : f + fc, :], m))
        acc[f : f + fc, :] += dot_nt(hi, hhi) + dot_nt(hi, hlo) + dot_nt(lo, hhi)

    @pl.when(i == steps - 1)
    def _():
        accn[...] = acc[...].T
        rows = atoms // n_out
        for s, o in enumerate(outs):
            target = lax.rem(idx[0] + s, n_dev) if n_out > 1 else 0
            at = rows_at(target, rows)
            o[:, :bins] = accn[at, :]
            o[:, bins:] = row_acc[at, :]


def call_second(idx, spectrum, hown, hoth, nown, noth, massa, massb, wt3, n_out, n_dev, block=1024, fc=256):
    bins, frames = spectrum.shape
    half = hown.shape[0]
    atoms = 2 * half
    block = min(block, frames)
    part = lambda r: pl.BlockSpec((r, block), lambda i: (0, i))
    whole = lambda a: pl.BlockSpec(a, lambda i: (0, 0))
    return pl.pallas_call(
        functools.partial(second_kernel, n_out=n_out, n_dev=n_dev, fc=fc, steps=frames // block),
        grid=(frames // block,),
        in_specs=[
            pl.BlockSpec(memory_space=pltpu.SMEM),
            part(bins),
            part(half),
            part(half),
            part(atoms),
            part(atoms),
            whole((atoms, 128)),
            whole((atoms, 128)),
            whole((bins, 3 * atoms)),
        ],
        out_specs=[part(half)] + [whole((atoms // n_out, bins + 128))] * n_out,
        out_shape=[jax.ShapeDtypeStruct((half, frames), f32)]
        + [jax.ShapeDtypeStruct((atoms // n_out, bins + 128), f32)] * n_out,
        scratch_shapes=[
            pltpu.VMEM((atoms, block), f32),
            pltpu.VMEM((bins, atoms), f32),
            pltpu.VMEM((atoms, 128), f32),
            pltpu.VMEM((atoms, bins), f32),
        ],
        compiler_params=pltpu.CompilerParams(vmem_limit_bytes=VMEM_LIMIT),
    )(idx, spectrum, hown, hoth, nown, noth, massa, massb, wt3)


def body(spectrum, atoms_by_bin, activations, *, n_dev):
    swap = [(0, 1), (1, 0)]
    idx = jnp.stack([lax.axis_index("frames"), lax.axis_index("bins")]).astype(jnp.int32)
    bins = spectrum.shape[0]
    rows = atoms_by_bin.shape[0]
    direct = n_dev <= 8 and rows % 16 == 0
    shift = lambda x, s: lax.ppermute(x, "frames", [(i, (i + s) % n_dev) for i in range(n_dev)])
    if direct:
        ws = [atoms_by_bin] + [shift(atoms_by_bin, s) for s in range(1, n_dev)]
    else:
        ws = [lax.all_gather(atoms_by_bin, "frames", axis=0, tiled=True)]
    other = lax.ppermute(activations, "bins", swap)
    numer, wt3, mass = call_first(idx, spectrum, activations, other, ws, n_dev)
    numer_other = lax.ppermute(numer, "bins", swap)
    mass_other = lax.ppermute(mass, "bins", swap)
    n_out = n_dev if direct else 1
    fresh, *parts = call_second(
        idx, spectrum, activations, other, numer, numer_other, mass, mass_other, wt3, n_out, n_dev
    )
    if direct:
        total = parts[0]
        for s in range(1, n_dev):
            total = total + shift(parts[s], s)
    else:
        total = lax.psum_scatter(parts[0], "frames", scatter_dimension=0, tiled=True)
    return fresh, atoms_by_bin * total[:, :bins] / total[:, bins : bins + 1]


def solution(mesh):
    return jax.shard_map(
        functools.partial(body, n_dev=mesh.shape["frames"]),
        mesh=mesh,
        in_specs=(P("bins", ("groups", "frames")), P("frames", ("groups", "bins")), P("bins", ("groups", "frames"))),
        out_specs=(P("bins", ("groups", "frames")), P("frames", ("groups", "bins"))),
        check_vma=False,
    )
```

```python
import functools

import jax
import jax.numpy as jnp
from jax import lax
from jax.experimental import pallas as pl
from jax.experimental.pallas import tpu as pltpu
from jax.sharding import PartitionSpec as P

f32, bf16 = jnp.float32, jnp.bfloat16
WHOLE = pl.BlockSpec(memory_space=pltpu.VMEM)
SCALARS = pl.BlockSpec(memory_space=pltpu.SMEM)
PARAMS = pltpu.CompilerParams(vmem_limit_bytes=36 * 2**20)
CROSS = 6


def split(x):
    hi = x.astype(bf16)
    return hi, (x - hi.astype(f32)).astype(bf16)


def dot(a, b):
    return jnp.dot(a, b, preferred_element_type=f32)


def dot_nt(a, b):
    return lax.dot_general(a, b, (((1,), (1,)), ((), ())), preferred_element_type=f32)


def rows_at(start, rows):
    return pl.ds(pl.multiple_of(start * rows, rows), rows)


def prepare_activations(idx, hown, hoth, h2):
    half = hown.shape[0]
    for place, old in ((idx[1], hown), (1 - idx[1], hoth)):
        hi, lo = split(old[...])
        h2[rows_at(place, half), :] = hi
        h2[rows_at(place + 2, half), :] = lo


def prepare_basis(idx, *refs, first):
    *ws, w2, wt, mass = refs
    rows = ws[0].shape[0]
    half = len(ws) * rows
    for s, w in enumerate(ws):
        x = w[...]
        hi, lo = split(x)
        place = (idx[0] ^ (s ^ first)) if len(ws) > 1 else 0
        w2[rows_at(place, rows), :] = hi
        w2[rows_at(place + half // rows, rows), :] = lo
        mass[rows_at(place, rows), :] = jnp.broadcast_to(jnp.sum(x, axis=1, keepdims=True), (rows, 128))
    wt[...] = w2[...].T


def first_kernel(h2, v, *refs, fc, nc):
    *parts, numer, rhi, rlo = refs
    w2, wt = parts[0::2], parts[1::2]
    bins, frames = v.shape
    atoms = h2.shape[0] // 2
    half = w2[0].shape[0] // 2
    whi = jnp.concatenate([w[:half, :] for w in w2], axis=0)
    wlo = jnp.concatenate([w[half:, :] for w in w2], axis=0)
    for n in range(0, frames, nc):
        at = slice(n, n + nc)
        hhi, hlo = h2[:atoms, at], h2[atoms:, at]
        h3 = jnp.concatenate([hhi, hhi, hlo], axis=0)
        for f in range(0, bins, fc):
            wthi = [w[f : f + fc, :half] for w in wt]
            wtlo = [w[f : f + fc, half:] for w in wt]
            m = dot(jnp.concatenate(wthi + wtlo + wthi, axis=1), h3)
            hi, lo = split(v[f : f + fc, at] / m)
            rhi[f : f + fc, at] = hi
            rlo[f : f + fc, at] = lo
        numer[:, at] = dot(whi, rhi[:, at]) + dot(wlo, rhi[:, at]) + dot(whi, rlo[:, at])


def second_kernel(idx, v, hown, hoth, nown, noth, *refs, n_parts, n_out, fc, nc):
    wt = refs[:n_parts]
    masses = refs[n_parts : 3 * n_parts]
    newact = refs[3 * n_parts]
    outs = refs[3 * n_parts + 1 : 3 * n_parts + 1 + n_out]
    h, acc, mass, row_mass = refs[3 * n_parts + 1 + n_out :]
    bins, frames = v.shape
    atoms = h.shape[0]
    half = hown.shape[0]
    part = atoms // n_parts
    for p in range(n_parts):
        mass[p * part : (p + 1) * part, :] = masses[p][...] + masses[n_parts + p][...]
    own, oth = rows_at(idx[1], half), rows_at(1 - idx[1], half)
    sums = None
    for n in range(0, frames, nc):
        at = slice(n, n + nc)
        fresh = hown[:, at] * (nown[own, at] + noth[own, at]) / mass[own, :1]
        newact[:, at] = fresh
        h[own, :] = fresh
        h[oth, :] = hoth[:, at] * (nown[oth, at] + noth[oth, at]) / mass[oth, :1]
        fresh = h[...]
        hhi, hlo = split(fresh)
        h3 = jnp.concatenate([hhi, hhi, hlo], axis=0)
        row = jnp.sum(fresh, axis=1, keepdims=True)
        sums = row if sums is None else sums + row
        for f in range(0, bins, fc):
            wthi = [w[f : f + fc, :part] for w in wt]
            wtlo = [w[f : f + fc, part:] for w in wt]
            m = dot(jnp.concatenate(wthi + wtlo + wthi, axis=1), h3)
            hi, lo = split(v[f : f + fc, at] / m)
            term = dot_nt(hhi, hi) + dot_nt(hlo, hi) + dot_nt(hhi, lo)
            if n == 0:
                acc[:, f : f + fc] = term
            else:
                acc[:, f : f + fc] += term
    row_mass[...] = jnp.broadcast_to(sums, row_mass.shape)
    if n_out == 1:
        outs[0][:, :bins] = acc[...]
        outs[0][:, bins:] = row_mass[...]
        return
    rows = atoms // n_out
    lane = lax.broadcasted_iota(jnp.int32, (8, 128), 1) // (1024 // rows)
    for s, o in enumerate(outs):
        place = (idx[0] ^ (s & 3)) + (s & 4)
        base = pl.multiple_of(place * rows, rows)
        packed = jnp.zeros((8, 128), f32)
        for i in range(rows // 8):
            at = pl.ds(base + 8 * i, 8)
            packed = jnp.where(lane == i, row_mass[at, :], packed)
            for j in range(bins // 128):
                k = 8 * (i * (bins // 128) + j)
                o[k : k + 8, :] = acc[at, 128 * j : 128 * (j + 1)]
        o[rows * bins // 128 :, :] = packed


def last_kernel(old, total, more, new):
    rows, bins = old.shape
    x = total[rows * bins // 128 :, :] + more[rows * bins // 128 :, :]
    for i in range(rows // 8):
        lane = i * (1024 // rows)
        mass = x[:, lane : lane + 1]
        for j in range(bins // 128):
            k = 8 * (i * (bins // 128) + j)
            at = (slice(8 * i, 8 * i + 8), slice(128 * j, 128 * (j + 1)))
            new[at] = old[at] * (total[k : k + 8, :] + more[k : k + 8, :]) / mass


def call(kernel, ins, outs, scratch=(), scalars=False):
    in_specs = [WHOLE] * len(ins)
    if scalars:
        in_specs[0] = SCALARS
    return pl.pallas_call(
        kernel,
        in_specs=in_specs,
        out_specs=[WHOLE] * len(outs),
        out_shape=[jax.ShapeDtypeStruct(*o) for o in outs],
        scratch_shapes=[pltpu.VMEM(*s) for s in scratch],
        compiler_params=PARAMS,
    )(*ins)


def hop(x, step):
    return lax.ppermute(x, "frames", [(i, i ^ step) for i in range(8)])


def body(spectrum, atoms_by_bin, activations, *, n_dev):
    swap = lambda x: lax.ppermute(x, "bins", [(0, 1), (1, 0)])
    bins, frames = spectrum.shape
    half = activations.shape[0]
    atoms = 2 * half
    rows = atoms_by_bin.shape[0]
    cube = n_dev == 8 and rows % 16 == 0
    place, core = lax.axis_index("frames"), lax.axis_index("bins")
    idx = jnp.stack([place & 3, core ^ (place >> 2)] if cube else [place, core]).astype(jnp.int32)

    def prepare(ws, first):
        k = sum(w.shape[0] for w in ws)
        return call(
            functools.partial(prepare_basis, first=first),
            [idx, *ws],
            [((2 * k, bins), bf16), ((bins, 2 * k), bf16), ((k, 128), f32)],
            scalars=True,
        )

    if cube:
        far = hop(atoms_by_bin, CROSS)
        near = [hop(atoms_by_bin, s) for s in (1, 2, 3)]
        fars = [hop(far, s) for s in (1, 2, 3)]
        basis = [prepare([atoms_by_bin, *near], 0), prepare([far, *fars], CROSS & 3)]
    else:
        basis = [prepare([lax.all_gather(atoms_by_bin, "frames", axis=0, tiled=True)], 0)]
    other = swap(activations)
    (h2,) = call(prepare_activations, [idx, activations, other], [((2 * atoms, frames), bf16)], scalars=True)
    w2, wt, mass = zip(*basis)
    (numer,) = call(
        functools.partial(first_kernel, fc=256, nc=512),
        [h2, spectrum, *[x for b in basis for x in b[:2]]],
        [((atoms, frames), f32)],
        scratch=[((bins, frames), bf16), ((bins, frames), bf16)],
    )
    mass_other = [swap(m) for m in mass]
    n_out = n_dev if cube else 1
    out = (rows * bins // 128 + 8, 128) if cube else (atoms, bins + 128)
    fresh, *parts = call(
        functools.partial(second_kernel, n_parts=len(basis), n_out=n_out, fc=256, nc=512),
        [idx, spectrum, activations, other, numer, swap(numer), *wt, *mass, *mass_other],
        [((half, frames), f32)] + [(out, f32)] * n_out,
        scratch=[((atoms, 512), f32), ((atoms, bins), f32), ((atoms, 128), f32), ((atoms, 128), f32)],
        scalars=True,
    )
    if cube:
        total = parts[CROSS]
        for s in (3, 2, 1):
            total = total + hop(parts[s ^ CROSS], s)
        more = hop(total, CROSS)
        total = parts[0]
        for s in (3, 2, 1):
            total = total + hop(parts[s], s)
        (new,) = call(last_kernel, [atoms_by_bin, total, more], [((rows, bins), f32)])
        return fresh, new
    total = lax.psum_scatter(parts[0], "frames", scatter_dimension=0, tiled=True)
    return fresh, atoms_by_bin * total[:, :bins] / total[:, bins : bins + 1]


def solution(mesh):
    return jax.shard_map(
        functools.partial(body, n_dev=mesh.shape["frames"]),
        mesh=mesh,
        in_specs=(P("bins", ("groups", "frames")), P("frames", ("groups", "bins")), P("bins", ("groups", "frames"))),
        out_specs=(P("bins", ("groups", "frames")), P("frames", ("groups", "bins"))),
        check_vma=False,
    )
```

```python
import functools

import jax
import jax.numpy as jnp
from jax import lax
from jax.experimental import pallas as pl
from jax.experimental.pallas import tpu as pltpu
from jax.sharding import PartitionSpec as P

f32, bf16 = jnp.float32, jnp.bfloat16
WHOLE = pl.BlockSpec(memory_space=pltpu.VMEM)
SCALARS = pl.BlockSpec(memory_space=pltpu.SMEM)
HBM = pl.BlockSpec(memory_space=pl.ANY)
GATHER_CROSS, REDUCE_CROSS = 6, 6
PIECES = 2
FC, NC = 256, 512


def split(x):
    hi = x.astype(bf16)
    return hi, (x - hi.astype(f32)).astype(bf16)


def dot(a, b):
    return jnp.dot(a, b, preferred_element_type=f32)


def dot_nt(a, b):
    return lax.dot_general(a, b, (((1,), (1,)), ((), ())), preferred_element_type=f32)


def rows_at(start, rows):
    return pl.ds(pl.multiple_of(start * rows, rows), rows)


def pack(columns, rows):
    lane = lax.broadcasted_iota(jnp.int32, (8, 128), 1) // (1024 // rows)
    tile = jnp.zeros((8, 128), f32)
    for i in range(rows // 8):
        tile = jnp.where(lane == i, columns(8 * i), tile)
    return tile


def unpack(tile, i, rows):
    lane = i * (1024 // rows)
    return jnp.broadcast_to(tile[:, lane : lane + 1], (8, 128))


def prepare(idx, ws, w2, wt, mass, first):
    rows = ws[0].shape[0]
    half = len(ws) * rows
    for s, w in enumerate(ws):
        x = w[...]
        hi, lo = split(x)
        place = (idx[0] ^ (s ^ first)) if len(ws) > 1 else 0
        w2[rows_at(place, rows), :] = hi
        w2[rows_at(place + half // rows, rows), :] = lo
        mass[rows_at(place, rows), :] = jnp.broadcast_to(jnp.sum(x, axis=1, keepdims=True), (rows, 128))
    wt[...] = w2[...].T


def prepare_kernel(idx, *refs):
    *ws, w2, wt, mass = refs
    prepare(idx, ws, w2, wt, mass, 0)


def order_kernel(idx, hown, hoth, h, h2):
    half = hown.shape[0]
    for place, old in ((idx[1], hown), (1 - idx[1], hoth)):
        x = old[...]
        hi, lo = split(x)
        h[rows_at(place, half), :] = x
        h2[rows_at(place, half), :] = hi
        h2[rows_at(place + 2, half), :] = lo


def by_three(parts, rows):
    half = parts[0].shape[1] // 2
    hi = [w[rows, :half] for w in parts]
    lo = [w[rows, half:] for w in parts]
    return jnp.concatenate(hi + lo + hi, axis=1)


def first_kernel(idx, v, h2, *refs, start, n_parts, masses, raw):
    refs = list(refs)
    take = lambda n: [refs.pop(0) for _ in range(n)]
    w2, wt = take(n_parts), take(n_parts)
    mass, ws, (numer,) = take(masses), take(raw), take(1)
    if raw:
        made = take(3)
        prepare(idx, ws, *made, GATHER_CROSS & 3)
        w2.append(made[0])
        wt.append(made[1])
        mass.append(made[2])
    rhi, rlo = refs
    bins, frames = rhi.shape
    atoms = h2.shape[0] // 2
    whi = jnp.concatenate([w[: w.shape[0] // 2, :] for w in w2], axis=0)
    wlo = jnp.concatenate([w[w.shape[0] // 2 :, :] for w in w2], axis=0)
    for n in range(0, frames, NC):
        at, src = slice(n, n + NC), slice(start + n, start + n + NC)
        h3 = jnp.concatenate([h2[:atoms, src], h2[:atoms, src], h2[atoms:, src]], axis=0)
        for f in range(0, bins, FC):
            m = dot(by_three(wt, slice(f, f + FC)), h3)
            hi, lo = split(v[f : f + FC, src] / m)
            rhi[f : f + FC, at] = hi
            rlo[f : f + FC, at] = lo
        numer[:atoms, at] = dot(whi, rhi[:, at]) + dot(wlo, rhi[:, at]) + dot(whi, rlo[:, at])
    if mass:
        part = mass[0].shape[0]
        numer[atoms:, :] = jnp.zeros((8, frames), f32)
        numer[atoms:, :128] = pack(lambda i: mass[i // part][i % part : i % part + 8, :], atoms)


def second_kernel(idx, v, h, mine, theirs, nown, noth, *refs, start, n_parts, before, n_out):
    refs = list(refs)
    take = lambda n: [refs.pop(0) for _ in range(n)]
    wt = take(n_parts)
    if before:
        acc_in, row_in, _ = take(3)
    (newact,) = take(1)
    outs = take(max(n_out, 2) if n_out != 1 else 1)
    fresh_own, f2, rhi, rlo, acc, scale, o_sems = refs
    bins, frames = rhi.shape
    atoms = h.shape[0]
    half = atoms // 2
    tile = 1.0 / (mine[atoms:, :128] + theirs[atoms:, :128])
    for i in range(atoms // 8):
        scale[8 * i : 8 * i + 8, :] = unpack(tile, i, atoms)
    sums = row_in[:, :1] if before else None
    written = []
    for n in range(0, frames, NC):
        at, src = slice(n, n + NC), slice(start + n, start + n + NC)
        fresh = h[:, src] * (nown[:atoms, at] + noth[:atoms, at]) * scale[:, :1]
        fresh_own[:, at] = fresh
        hhi, hlo = split(fresh)
        f2[:atoms, at] = hhi
        f2[atoms:, at] = hlo
        row = jnp.sum(fresh, axis=1, keepdims=True)
        sums = row if sums is None else sums + row
        written.append(
            pltpu.make_async_copy(
                fresh_own.at[rows_at(idx[1], half), pl.ds(n, NC)],
                newact.at[:, pl.ds(start + n, NC)],
                o_sems.at[n // NC],
            )
        )
        written[-1].start()
    for n in range(0, frames, NC):
        at, src = slice(n, n + NC), slice(start + n, start + n + NC)
        h3 = jnp.concatenate([f2[:atoms, at], f2[:atoms, at], f2[atoms:, at]], axis=0)
        for f in range(0, bins, FC):
            m = dot(by_three(wt, slice(f, f + FC)), h3)
            hi, lo = split(v[f : f + FC, src] / m)
            rhi[f : f + FC, at] = hi
            rlo[f : f + FC, at] = lo
    total = dot_nt(f2[:atoms, :], rhi[...]) + dot_nt(f2[atoms:, :], rhi[...]) + dot_nt(f2[:atoms, :], rlo[...])
    if before:
        total = total + acc_in[...]
    row_mass = jnp.broadcast_to(sums, (atoms, 128))
    if n_out == 0:
        outs[0][...] = total
        outs[1][...] = row_mass
    elif n_out == 1:
        outs[0][:, :bins] = total
        outs[0][:, bins:] = row_mass
    else:
        acc[...] = total
        scale[...] = row_mass
        rows = atoms // n_out
        for s, o in enumerate(outs):
            place = (idx[0] ^ (s & 3)) + (s & 4)
            base = pl.multiple_of(place * rows, rows)
            for i in range(rows // 8):
                for j in range(bins // 128):
                    k = 8 * (i * (bins // 128) + j)
                    o[k : k + 8, :] = acc[pl.ds(base + 8 * i, 8), 128 * j : 128 * (j + 1)]
            o[rows * bins // 128 :, :] = pack(lambda i: scale[pl.ds(base + i, 8), :], rows)
    for copy in written:
        copy.wait()


def last_kernel(old, total, more, new):
    rows, bins = old.shape
    x = 1.0 / (total[rows * bins // 128 :, :] + more[rows * bins // 128 :, :])
    for i in range(rows // 8):
        scale = unpack(x, i, rows)
        for j in range(bins // 128):
            k = 8 * (i * (bins // 128) + j)
            at = (slice(8 * i, 8 * i + 8), slice(128 * j, 128 * (j + 1)))
            new[at] = old[at] * (total[k : k + 8, :] + more[k : k + 8, :]) * scale


def call(kernel, ins, outs, scratch=(), in_specs=(), out_specs=(), aliases=None, mib=28, flops=0):
    return pl.pallas_call(
        kernel,
        in_specs=list(in_specs) + [WHOLE] * (len(ins) - len(in_specs)),
        out_specs=list(out_specs) + [WHOLE] * (len(outs) - len(out_specs)),
        out_shape=[jax.ShapeDtypeStruct(*o) for o in outs],
        scratch_shapes=[pltpu.VMEM(*s) if isinstance(s, tuple) else s for s in scratch],
        input_output_aliases=aliases or {},
        compiler_params=pltpu.CompilerParams(vmem_limit_bytes=mib * 2**20),
        cost_estimate=pl.CostEstimate(flops=flops, bytes_accessed=0, transcendentals=0) if flops else None,
    )(*ins)


def hop(x, step):
    return lax.ppermute(x, "frames", [(i, i ^ step) for i in range(8)])


def body(spectrum, atoms_by_bin, activations, *, n_dev):
    swap = lambda x: lax.ppermute(x, "bins", [(0, 1), (1, 0)])
    bins, frames = spectrum.shape
    half = activations.shape[0]
    atoms = 2 * half
    rows = atoms_by_bin.shape[0]
    cube = n_dev == 8 and rows % 16 == 0
    place, core = lax.axis_index("frames"), lax.axis_index("bins")
    idx = jnp.stack([place & 3, core ^ (place >> 2)] if cube else [place, core]).astype(jnp.int32)
    size = frames // PIECES

    def basis_outs(k):
        return [((2 * k, bins), bf16), ((bins, 2 * k), bf16), ((k, 128), f32)]

    other = swap(activations)
    raw = []
    if cube:
        far = hop(atoms_by_bin, GATHER_CROSS)
        near = [hop(atoms_by_bin, s) for s in (1, 2, 3)]
        raw = [far] + [hop(far, s) for s in (1, 2, 3)]
        near = [atoms_by_bin, *near]
    else:
        near = [lax.all_gather(atoms_by_bin, "frames", axis=0, tiled=True)]
    h, h2 = call(
        order_kernel,
        [idx, activations, other],
        [((atoms, frames), f32), ((2 * atoms, frames), bf16)],
        in_specs=[SCALARS],
        mib=16,
        flops=10**9,
    )
    k = sum(w.shape[0] for w in near)
    w2, wt, mass = call(prepare_kernel, [idx, *near], basis_outs(k), in_specs=[SCALARS], mib=16, flops=10**10)
    w2, wt, mass = [w2], [wt], [mass]
    numers = []
    for p in range(PIECES):
        numer, *made = call(
            functools.partial(first_kernel, start=p * size, n_parts=len(wt), masses=len(mass), raw=len(raw)),
            [idx, spectrum, h2, *w2, *wt, *mass, *raw],
            [((atoms + 8 * (p == 0), size), f32)] + (basis_outs(atoms - k) if raw else []),
            scratch=[((bins, size), bf16), ((bins, size), bf16)],
            in_specs=[SCALARS],
        )
        if raw:
            w2.append(made[0])
            wt.append(made[1])
        raw, mass = [], []
        numers.append((numer, swap(numer)))
    n_out = n_dev if cube else 1
    block = (rows * bins // 128 + 8, 128) if cube else (atoms, bins + 128)
    carried = []
    for p in range(PIECES):
        final = p == PIECES - 1
        ins = [idx, spectrum, h, *numers[0], *numers[p], *wt]
        fresh, *carried = call(
            functools.partial(
                second_kernel, start=p * size, n_parts=len(wt), before=p > 0, n_out=n_out if final else 0
            ),
            ins + carried + ([fresh] if p else []),
            [((half, frames), f32)]
            + ([(block, f32)] * n_out if final else [((atoms, bins), f32), ((atoms, 128), f32)]),
            scratch=[
                ((atoms, size), f32),
                ((2 * atoms, size), bf16),
                ((bins, size), bf16),
                ((bins, size), bf16),
                ((atoms, bins), f32),
                ((atoms, 128), f32),
                pltpu.SemaphoreType.DMA((size // NC,)),
            ],
            in_specs=[SCALARS] + ([WHOLE] * (len(ins) + 1) + [HBM] if p else []),
            out_specs=[HBM],
            aliases={len(ins) + 2: 0} if p else None,
        )
    parts = carried
    if cube:
        total = parts[REDUCE_CROSS]
        for s in (3, 2, 1):
            total = total + hop(parts[s ^ REDUCE_CROSS], s)
        more = hop(total, REDUCE_CROSS)
        total = parts[0]
        for s in (3, 2, 1):
            total = total + hop(parts[s], s)
        (new,) = call(last_kernel, [atoms_by_bin, total, more], [((rows, bins), f32)], mib=16)
        return fresh, new
    total = lax.psum_scatter(parts[0], "frames", scatter_dimension=0, tiled=True)
    return fresh, atoms_by_bin * total[:, :bins] / total[:, bins : bins + 1]


def solution(mesh):
    return jax.shard_map(
        functools.partial(body, n_dev=mesh.shape["frames"]),
        mesh=mesh,
        in_specs=(P("bins", ("groups", "frames")), P("frames", ("groups", "bins")), P("bins", ("groups", "frames"))),
        out_specs=(P("bins", ("groups", "frames")), P("frames", ("groups", "bins"))),
        check_vma=False,
    )
```

```python
import functools

import jax
import jax.numpy as jnp
from jax import lax
from jax.experimental import pallas as pl
from jax.experimental.pallas import tpu as pltpu
from jax.sharding import PartitionSpec as P

f32, bf16 = jnp.float32, jnp.bfloat16
WHOLE = pl.BlockSpec(memory_space=pltpu.VMEM)
HBM = pl.BlockSpec(memory_space=pl.ANY)
GATHER_CROSS, REDUCE_CROSS = 4, 6
PIECES = 2
FC, NC = 256, 512


def split(x):
    hi = x.astype(bf16)
    return hi, (x - hi.astype(f32)).astype(bf16)


def dot(a, b):
    return jnp.dot(a, b, preferred_element_type=f32)


def dot_nt(a, b):
    return lax.dot_general(a, b, (((1,), (1,)), ((), ())), preferred_element_type=f32)


def rows_at(start, rows):
    return pl.ds(pl.multiple_of(start * rows, rows), rows)


def pack(columns, rows):
    lane = lax.broadcasted_iota(jnp.int32, (8, 128), 1) // (1024 // rows)
    tile = jnp.zeros((8, 128), f32)
    for i in range(rows // 8):
        tile = jnp.where(lane == i, columns(8 * i), tile)
    return tile


def unpack(tile, i, rows):
    lane = i * (1024 // rows)
    return jnp.broadcast_to(tile[:, lane : lane + 1], (8, 128))


def whereabouts(cube):
    place, core = lax.axis_index("frames"), lax.axis_index("bins")
    return (place & 3, core ^ (place >> 2)) if cube else (place, core)


def prepare(ws, w2, wt, mass, first):
    rows = ws[0].shape[0]
    half = len(ws) * rows
    place_of_mine = whereabouts(True)[0]
    for s, w in enumerate(ws):
        x = w[...]
        hi, lo = split(x)
        place = (place_of_mine ^ (s ^ first)) if len(ws) > 1 else 0
        w2[rows_at(place, rows), :] = hi
        w2[rows_at(place + half // rows, rows), :] = lo
        mass[rows_at(place, rows), :] = jnp.broadcast_to(jnp.sum(x, axis=1, keepdims=True), (rows, 128))
    wt[...] = w2[...].T


def prepare_kernel(*refs):
    *ws, w2, wt, mass = refs
    prepare(ws, w2, wt, mass, 0)


def own_kernel(hown, atoms, h, h2, kept, *, cube):
    place_rows(hown, h, h2, whereabouts(cube)[1])
    kept[...] = atoms[...]


def other_kernel(hoth, _h, _h2, h, h2, *, cube):
    place_rows(hoth, h, h2, 1 - whereabouts(cube)[1])


def place_rows(old, h, h2, place):
    half = old.shape[0]
    x = old[...]
    hi, lo = split(x)
    h[rows_at(place, half), :] = x
    h2[rows_at(place, half), :] = hi
    h2[rows_at(place + 2, half), :] = lo


def by_three(parts, rows):
    half = parts[0].shape[1] // 2
    hi = [w[rows, :half] for w in parts]
    lo = [w[rows, half:] for w in parts]
    return jnp.concatenate(hi + lo + hi, axis=1)


def first_kernel(v, h2, *refs, start, n_parts, masses, raw):
    refs = list(refs)
    take = lambda n: [refs.pop(0) for _ in range(n)]
    w2, wt = take(n_parts), take(n_parts)
    mass, ws, (numer,) = take(masses), take(raw), take(1)
    if raw:
        made = take(3)
        prepare(ws, *made, GATHER_CROSS & 3)
        w2.append(made[0])
        wt.append(made[1])
        mass.append(made[2])
    rhi, rlo = refs
    bins, frames = rhi.shape
    atoms = h2.shape[0] // 2
    whi = jnp.concatenate([w[: w.shape[0] // 2, :] for w in w2], axis=0)
    wlo = jnp.concatenate([w[w.shape[0] // 2 :, :] for w in w2], axis=0)
    for n in range(0, frames, NC):
        at, src = slice(n, n + NC), slice(start + n, start + n + NC)
        h3 = jnp.concatenate([h2[:atoms, src], h2[:atoms, src], h2[atoms:, src]], axis=0)
        for f in range(0, bins, FC):
            m = dot(by_three(wt, slice(f, f + FC)), h3)
            hi, lo = split(v[f : f + FC, src] / m)
            rhi[f : f + FC, at] = hi
            rlo[f : f + FC, at] = lo
        numer[:atoms, at] = dot(whi, rhi[:, at]) + dot(wlo, rhi[:, at]) + dot(whi, rlo[:, at])
    if mass:
        part = mass[0].shape[0]
        numer[atoms:, :] = jnp.zeros((8, frames), f32)
        numer[atoms:, :128] = pack(lambda i: mass[i // part][i % part : i % part + 8, :], atoms)


def second_kernel(v, h, mine, theirs, nown, noth, *refs, start, n_parts, before, n_out):
    refs = list(refs)
    take = lambda n: [refs.pop(0) for _ in range(n)]
    wt = take(n_parts)
    if before:
        acc_in, row_in, _ = take(3)
    (newact,) = take(1)
    outs = take(max(n_out, 2) if n_out != 1 else 1)
    fresh_own, f2, rhi, rlo, acc, scale, o_sems = refs
    place_of_mine, half_of_mine = whereabouts(n_parts > 1)
    bins, frames = rhi.shape
    atoms = h.shape[0]
    half = atoms // 2
    tile = 1.0 / (mine[atoms:, :128] + theirs[atoms:, :128])
    for i in range(atoms // 8):
        scale[8 * i : 8 * i + 8, :] = unpack(tile, i, atoms)
    sums = row_in[:, :1] if before else None
    written = []
    for n in range(0, frames, NC):
        at, src = slice(n, n + NC), slice(start + n, start + n + NC)
        fresh = h[:, src] * (nown[:atoms, at] + noth[:atoms, at]) * scale[:, :1]
        fresh_own[:, at] = fresh
        hhi, hlo = split(fresh)
        f2[:atoms, at] = hhi
        f2[atoms:, at] = hlo
        row = jnp.sum(fresh, axis=1, keepdims=True)
        sums = row if sums is None else sums + row
        written.append(
            pltpu.make_async_copy(
                fresh_own.at[rows_at(half_of_mine, half), pl.ds(n, NC)],
                newact.at[:, pl.ds(start + n, NC)],
                o_sems.at[n // NC],
            )
        )
        written[-1].start()
    for n in range(0, frames, NC):
        at, src = slice(n, n + NC), slice(start + n, start + n + NC)
        h3 = jnp.concatenate([f2[:atoms, at], f2[:atoms, at], f2[atoms:, at]], axis=0)
        for f in range(0, bins, FC):
            m = dot(by_three(wt, slice(f, f + FC)), h3)
            hi, lo = split(v[f : f + FC, src] / m)
            rhi[f : f + FC, at] = hi
            rlo[f : f + FC, at] = lo
    total = dot_nt(f2[:atoms, :], rhi[...]) + dot_nt(f2[atoms:, :], rhi[...]) + dot_nt(f2[:atoms, :], rlo[...])
    if before:
        total = total + acc_in[...]
    row_mass = jnp.broadcast_to(sums, (atoms, 128))
    if n_out == 0:
        outs[0][...] = total
        outs[1][...] = row_mass
    elif n_out == 1:
        outs[0][:, :bins] = total
        outs[0][:, bins:] = row_mass
    else:
        acc[...] = total
        scale[...] = row_mass
        rows = atoms // n_out
        for s, o in enumerate(outs):
            place = (place_of_mine ^ (s & 3)) + (s & 4)
            base = pl.multiple_of(place * rows, rows)
            for i in range(rows // 8):
                for j in range(bins // 128):
                    k = 8 * (i * (bins // 128) + j)
                    o[k : k + 8, :] = acc[pl.ds(base + 8 * i, 8), 128 * j : 128 * (j + 1)]
            o[rows * bins // 128 :, :] = pack(lambda i: scale[pl.ds(base + i, 8), :], rows)
    for copy in written:
        copy.wait()


def last_kernel(old, total, more, new):
    rows, bins = old.shape
    x = 1.0 / (total[rows * bins // 128 :, :] + more[rows * bins // 128 :, :])
    for i in range(rows // 8):
        scale = unpack(x, i, rows)
        for j in range(bins // 128):
            k = 8 * (i * (bins // 128) + j)
            at = (slice(8 * i, 8 * i + 8), slice(128 * j, 128 * (j + 1)))
            new[at] = old[at] * (total[k : k + 8, :] + more[k : k + 8, :]) * scale


def call(kernel, ins, outs, scratch=(), in_specs=(), out_specs=(), aliases=None, mib=28, flops=0):
    return pl.pallas_call(
        kernel,
        in_specs=list(in_specs) + [WHOLE] * (len(ins) - len(in_specs)),
        out_specs=list(out_specs) + [WHOLE] * (len(outs) - len(out_specs)),
        out_shape=[jax.ShapeDtypeStruct(*o) for o in outs],
        scratch_shapes=[pltpu.VMEM(*s) if isinstance(s, tuple) else s for s in scratch],
        input_output_aliases=aliases or {},
        compiler_params=pltpu.CompilerParams(vmem_limit_bytes=mib * 2**20),
        cost_estimate=pl.CostEstimate(flops=flops, bytes_accessed=0, transcendentals=0) if flops else None,
    )(*ins)


def hop(x, step):
    return lax.ppermute(x, "frames", [(i, i ^ step) for i in range(8)])


def body(spectrum, atoms_by_bin, activations, *, n_dev):
    swap = lambda x: lax.ppermute(x, "bins", [(0, 1), (1, 0)])
    bins, frames = spectrum.shape
    half = activations.shape[0]
    atoms = 2 * half
    rows = atoms_by_bin.shape[0]
    cube = n_dev == 8 and rows % 16 == 0
    size = frames // PIECES

    def basis_outs(k):
        return [((2 * k, bins), bf16), ((bins, 2 * k), bf16), ((k, 128), f32)]

    ordered = [((atoms, frames), f32), ((2 * atoms, frames), bf16)]
    h, h2, kept = call(
        functools.partial(own_kernel, cube=cube),
        [activations, atoms_by_bin],
        ordered + [((rows, bins), f32)],
        mib=16,
        flops=10**10,
    )
    raw = []
    if cube:
        near = [hop(atoms_by_bin, s) for s in (1, 2, 3)]
        far = hop(atoms_by_bin, GATHER_CROSS)
        raw = [far] + [hop(far, s) for s in (1, 2, 3)]
        near = [kept, *near]
    else:
        near = [lax.all_gather(atoms_by_bin, "frames", axis=0, tiled=True)]
    h, h2 = call(
        functools.partial(other_kernel, cube=cube),
        [swap(activations), h, h2],
        ordered,
        aliases={1: 0, 2: 1},
        mib=16,
        flops=10**9,
    )
    k = sum(w.shape[0] for w in near)
    w2, wt, mass = call(prepare_kernel, near, basis_outs(k), mib=16, flops=10**10)
    w2, wt, mass = [w2], [wt], [mass]
    numers = []
    for p in range(PIECES):
        numer, *made = call(
            functools.partial(first_kernel, start=p * size, n_parts=len(wt), masses=len(mass), raw=len(raw)),
            [spectrum, h2, *w2, *wt, *mass, *raw],
            [((atoms + 8 * (p == 0), size), f32)] + (basis_outs(atoms - k) if raw else []),
            scratch=[((bins, size), bf16), ((bins, size), bf16)],
        )
        if raw:
            w2.append(made[0])
            wt.append(made[1])
        raw, mass = [], []
        numers.append((numer, swap(numer)))
    n_out = n_dev if cube else 1
    block = (rows * bins // 128 + 8, 128) if cube else (atoms, bins + 128)
    carried = []
    for p in range(PIECES):
        final = p == PIECES - 1
        ins = [spectrum, h, *numers[0], *numers[p], *wt]
        fresh, *carried = call(
            functools.partial(
                second_kernel, start=p * size, n_parts=len(wt), before=p > 0, n_out=n_out if final else 0
            ),
            ins + carried + ([fresh] if p else []),
            [((half, frames), f32)]
            + ([(block, f32)] * n_out if final else [((atoms, bins), f32), ((atoms, 128), f32)]),
            scratch=[
                ((atoms, size), f32),
                ((2 * atoms, size), bf16),
                ((bins, size), bf16),
                ((bins, size), bf16),
                ((atoms, bins), f32),
                ((atoms, 128), f32),
                pltpu.SemaphoreType.DMA((size // NC,)),
            ],
            in_specs=[WHOLE] * (len(ins) + 2) + [HBM] if p else [],
            out_specs=[HBM],
            aliases={len(ins) + 2: 0} if p else None,
        )
    parts = carried
    if cube:
        total = parts[REDUCE_CROSS]
        for s in (3, 2, 1):
            total = total + hop(parts[s ^ REDUCE_CROSS], s)
        more = hop(total, REDUCE_CROSS)
        total = parts[0]
        for s in (3, 2, 1):
            total = total + hop(parts[s], s)
        (new,) = call(last_kernel, [kept, total, more], [((rows, bins), f32)], mib=16)
        return fresh, new
    total = lax.psum_scatter(parts[0], "frames", scatter_dimension=0, tiled=True)
    return fresh, atoms_by_bin * total[:, :bins] / total[:, bins : bins + 1]


def solution(mesh):
    return jax.shard_map(
        functools.partial(body, n_dev=mesh.shape["frames"]),
        mesh=mesh,
        in_specs=(P("bins", ("groups", "frames")), P("frames", ("groups", "bins")), P("bins", ("groups", "frames"))),
        out_specs=(P("bins", ("groups", "frames")), P("frames", ("groups", "bins"))),
        check_vma=False,
    )
```

```python
import functools

import jax
import jax.numpy as jnp
from jax import lax
from jax.experimental import pallas as pl
from jax.experimental.pallas import tpu as pltpu
from jax.sharding import PartitionSpec as P

f32, bf16 = jnp.float32, jnp.bfloat16
WHOLE = pl.BlockSpec(memory_space=pltpu.VMEM)
HBM = pl.BlockSpec(memory_space=pl.ANY)
GATHER_CROSS, REDUCE_CROSS = 4, 6
PIECES = 2
FC, NC = 256, 512


def split(x):
    hi = x.astype(bf16)
    return hi, (x - hi.astype(f32)).astype(bf16)


def dot(a, b):
    return jnp.dot(a, b, preferred_element_type=f32)


def dot_nt(a, b):
    return lax.dot_general(a, b, (((1,), (1,)), ((), ())), preferred_element_type=f32)


def rows_at(start, rows):
    return pl.ds(pl.multiple_of(start * rows, rows), rows)


def pack(columns, rows):
    lane = lax.broadcasted_iota(jnp.int32, (8, 128), 1) // (1024 // rows)
    tile = jnp.zeros((8, 128), f32)
    for i in range(rows // 8):
        tile = jnp.where(lane == i, columns(8 * i), tile)
    return tile


def unpack(tile, i, rows):
    lane = i * (1024 // rows)
    return jnp.broadcast_to(tile[:, lane : lane + 1], (8, 128))


def whereabouts(cube):
    place, core = lax.axis_index("frames"), lax.axis_index("bins")
    return (place & 3, core ^ (place >> 2)) if cube else (place, core)


def prepare(ws, w2, wt, mass, first, columns):
    rows = ws[0].shape[0]
    half = len(ws) * rows
    place_of_mine = whereabouts(True)[0]
    for s, w in enumerate(ws):
        x = w[:, columns]
        hi, lo = split(x)
        place = (place_of_mine ^ (s ^ first)) if len(ws) > 1 else 0
        w2[rows_at(place, rows), columns] = hi
        w2[rows_at(place + half // rows, rows), columns] = lo
        total = sum(x[:, i : i + 128] for i in range(0, x.shape[1], 128))
        if columns.start:
            total = total + mass[rows_at(place, rows), :]
        if columns.stop == w.shape[1]:
            total = jnp.broadcast_to(jnp.sum(total, axis=1, keepdims=True), total.shape)
        mass[rows_at(place, rows), :] = total
    wt[columns, :] = w2[:, columns].T


def prepare_kernel(*refs):
    *ws, w2, wt, mass = refs
    prepare(ws, w2, wt, mass, 0, slice(0, wt.shape[0]))


def own_kernel(hown, atoms, h, h2, kept, *, cube):
    place_rows(hown, h, h2, whereabouts(cube)[1])
    kept[...] = atoms[...]


def other_kernel(hoth, _h, _h2, h, h2, *, cube):
    place_rows(hoth, h, h2, 1 - whereabouts(cube)[1])


def place_rows(old, h, h2, place):
    half = old.shape[0]
    x = old[...]
    hi, lo = split(x)
    h[rows_at(place, half), :] = x
    h2[rows_at(place, half), :] = hi
    h2[rows_at(place + 2, half), :] = lo


def hi_lo(parts, rows):
    half = parts[0].shape[1] // 2
    return [w[rows, :half] for w in parts], [w[rows, half:] for w in parts]


def by_three(parts, rows):
    hi, lo = hi_lo(parts, rows)
    return jnp.concatenate(hi + lo + hi, axis=1)


def near_kernel(wt, h2, model):
    half = wt.shape[1] // 2
    h = jnp.concatenate([h2[:half, :], h2[:half, :]], axis=0)
    for f in range(0, wt.shape[0], FC):
        model[f : f + FC, :] = dot(wt[f : f + FC, :], h)


def first_kernel(v, h2, *refs, start, n_parts, masses, raw, near):
    refs = list(refs)
    take = lambda n: [refs.pop(0) for _ in range(n)]
    (model,) = take(1) if near else (None,)
    w2, wt = take(n_parts), take(n_parts)
    mass, ws, (numer,) = take(masses), take(raw), take(1)
    if raw:
        made = take(3)
        w2.append(made[0])
        wt.append(made[1])
        mass.append(made[2])
    rhi, rlo = refs
    bins, frames = rhi.shape
    atoms = h2.shape[0] // 2
    for n in range(0, frames, NC):
        at, src = slice(n, n + NC), slice(start + n, start + n + NC)
        top = h2[atoms // 2 if near else 0 : atoms, src]
        h3 = jnp.concatenate([top, top, h2[atoms:, src]], axis=0)
        for f in range(0, bins, FC):
            rows = slice(f, f + FC)
            if raw and n == 0:
                prepare(ws, *made, GATHER_CROSS & 3, rows)
            if near:
                hi, lo = hi_lo(wt, rows)
                m = model[rows, src] + dot(jnp.concatenate([hi[1], lo[1], *hi], axis=1), h3)
            else:
                m = dot(by_three(wt, rows), h3)
            hi, lo = split(v[rows, src] / m)
            rhi[rows, at] = hi
            rlo[rows, at] = lo
        whi = jnp.concatenate([w[: w.shape[0] // 2, :] for w in w2], axis=0)
        wlo = jnp.concatenate([w[w.shape[0] // 2 :, :] for w in w2], axis=0)
        numer[:atoms, at] = dot(whi, rhi[:, at]) + dot(wlo, rhi[:, at]) + dot(whi, rlo[:, at])
    if mass:
        part = mass[0].shape[0]
        numer[atoms:, :] = jnp.zeros((8, frames), f32)
        numer[atoms:, :128] = pack(lambda i: mass[i // part][i % part : i % part + 8, :], atoms)


def second_kernel(v, h, mine, theirs, nown, noth, *refs, start, n_parts, before, n_out):
    refs = list(refs)
    take = lambda n: [refs.pop(0) for _ in range(n)]
    wt = take(n_parts)
    if before:
        acc_in, row_in, other_rhi, other_f2, _ = take(5)
    newact, acc, row_mass, rhi, f2 = take(5)
    outs = take(n_out)
    fresh, rlo, scale, cross, o_sems = refs
    bins, frames = rhi.shape
    atoms = h.shape[0]
    half = atoms // 2
    half_of_mine = whereabouts(n_parts > 1)[1]
    tile = 1.0 / (mine[atoms:, :128] + theirs[atoms:, :128])
    for i in range(atoms // 8):
        scale[8 * i : 8 * i + 8, :] = unpack(tile, i, atoms)
    sums = row_in[:, :1] if before else None
    written = []
    for n in range(0, frames, NC):
        at, src = slice(n, n + NC), slice(start + n, start + n + NC)
        x = h[:, src] * (nown[:atoms, at] + noth[:atoms, at]) * scale[:, :1]
        fresh[:, at] = x
        hi, lo = split(x)
        f2[:atoms, at] = hi
        f2[atoms:, at] = lo
        row = jnp.sum(x, axis=1, keepdims=True)
        sums = row if sums is None else sums + row
        written.append(
            pltpu.make_async_copy(
                fresh.at[rows_at(half_of_mine, half), pl.ds(n, NC)],
                newact.at[:, pl.ds(start + n, NC)],
                o_sems.at[n // NC],
            )
        )
        written[-1].start()
        h3 = jnp.concatenate([f2[:atoms, at], f2[:atoms, at], f2[atoms:, at]], axis=0)
        for f in range(0, bins, FC):
            m = dot(by_three(wt, slice(f, f + FC)), h3)
            hi, lo = split(v[f : f + FC, src] / m)
            rhi[f : f + FC, at] = hi
            rlo[f : f + FC, at] = lo
    row_mass[...] = jnp.broadcast_to(sums, (atoms, 128))
    total = dot_nt(f2[:atoms, :], rlo[...])
    if before:
        total = total + acc_in[...]
        acc[...] = total[:half, :]
        cross[...] = total[half:, :] + by_high(half, (f2, rhi), (other_f2, other_rhi))
        write_blocks(outs, cross, row_mass, half, atoms // 8)
    else:
        acc[...] = total
    for copy in written:
        copy.wait()


def by_high(start, *pairs):
    total = None
    for f2, rhi in pairs:
        atoms = f2.shape[0] // 2
        half = atoms // 2
        rows = [f2[start : start + half, :], f2[atoms + start : atoms + start + half, :]]
        x = dot_nt(jnp.concatenate(rows, axis=0), rhi[...])
        total = x if total is None else total + x
    return total[: total.shape[0] // 2, :] + total[total.shape[0] // 2 :, :]


def write_blocks(outs, acc, row_mass, start, rows):
    bins = acc.shape[1]
    if len(outs) == 1:
        outs[0][:, :bins] = acc[...]
        outs[0][:, bins:] = row_mass[start : start + acc.shape[0], :]
        return
    place_of_mine = whereabouts(True)[0]
    for s, o in enumerate(outs):
        base = pl.multiple_of((place_of_mine ^ s) * rows, rows)
        for i in range(rows // 8):
            for j in range(bins // 128):
                k = 8 * (i * (bins // 128) + j)
                o[k : k + 8, :] = acc[pl.ds(base + 8 * i, 8), 128 * j : 128 * (j + 1)]
        o[rows * bins // 128 :, :] = pack(lambda i: row_mass[pl.ds(start + base + i, 8), :], rows)


def third_kernel(acc, row_mass, rhi_a, f2_a, rhi_b, f2_b, *refs):
    *outs, own = refs
    own[...] = acc[...] + by_high(0, (f2_b, rhi_b), (f2_a, rhi_a))
    write_blocks(outs, own, row_mass, 0, f2_a.shape[0] // 16)


def last_kernel(old, total, more, new):
    rows, bins = old.shape
    x = 1.0 / (total[rows * bins // 128 :, :] + more[rows * bins // 128 :, :])
    for i in range(rows // 8):
        scale = unpack(x, i, rows)
        for j in range(bins // 128):
            k = 8 * (i * (bins // 128) + j)
            at = (slice(8 * i, 8 * i + 8), slice(128 * j, 128 * (j + 1)))
            new[at] = old[at] * (total[k : k + 8, :] + more[k : k + 8, :]) * scale


def call(kernel, ins, outs, scratch=(), in_specs=(), out_specs=(), aliases=None, mib=28, flops=0):
    return pl.pallas_call(
        kernel,
        in_specs=list(in_specs) + [WHOLE] * (len(ins) - len(in_specs)),
        out_specs=list(out_specs) + [WHOLE] * (len(outs) - len(out_specs)),
        out_shape=[jax.ShapeDtypeStruct(*o) for o in outs],
        scratch_shapes=[pltpu.VMEM(*s) if isinstance(s, tuple) else s for s in scratch],
        input_output_aliases=aliases or {},
        compiler_params=pltpu.CompilerParams(vmem_limit_bytes=mib * 2**20),
        cost_estimate=pl.CostEstimate(flops=flops, bytes_accessed=0, transcendentals=0) if flops else None,
    )(*ins)


def hop(x, step):
    return lax.ppermute(x, "frames", [(i, i ^ step) for i in range(8)])


def body(spectrum, atoms_by_bin, activations, *, n_dev):
    swap = lambda x: lax.ppermute(x, "bins", [(0, 1), (1, 0)])
    bins, frames = spectrum.shape
    half = activations.shape[0]
    atoms = 2 * half
    rows = atoms_by_bin.shape[0]
    cube = n_dev == 8 and rows % 16 == 0
    size = frames // PIECES

    def basis_outs(k):
        return [((2 * k, bins), bf16), ((bins, 2 * k), bf16), ((k, 128), f32)]

    ordered = [((atoms, frames), f32), ((2 * atoms, frames), bf16)]
    h, h2, kept = call(
        functools.partial(own_kernel, cube=cube),
        [activations, atoms_by_bin],
        ordered + [((rows, bins), f32)],
        mib=16,
        flops=10**10,
    )
    raw = []
    if cube:
        near = [hop(atoms_by_bin, s) for s in (1, 2, 3)]
        far = hop(atoms_by_bin, GATHER_CROSS)
        raw = [far] + [hop(far, s) for s in (1, 2, 3)]
        near = [kept, *near]
    else:
        near = [lax.all_gather(atoms_by_bin, "frames", axis=0, tiled=True)]
    h, h2 = call(
        functools.partial(other_kernel, cube=cube),
        [swap(activations), h, h2],
        ordered,
        aliases={1: 0, 2: 1},
        mib=16,
        flops=10**9,
    )
    k = sum(w.shape[0] for w in near)
    w2, wt, mass = call(prepare_kernel, near, basis_outs(k), mib=16, flops=10**10)
    model = call(near_kernel, [wt, h2], [((bins, frames), f32)], mib=16, flops=10**10) if cube else []
    w2, wt, mass = [w2], [wt], [mass]
    numers = []
    for p in range(PIECES):
        numer, *made = call(
            functools.partial(first_kernel, start=p * size, n_parts=len(wt), masses=len(mass), raw=len(raw), near=cube),
            [spectrum, h2, *model, *w2, *wt, *mass, *raw],
            [((atoms + 8 * (p == 0), size), f32)] + (basis_outs(atoms - k) if raw else []),
            scratch=[((bins, size), bf16), ((bins, size), bf16)],
        )
        if raw:
            w2.append(made[0])
            wt.append(made[1])
        raw, mass = [], []
        numers.append((numer, swap(numer)))
    n_out = 4 if cube else 1
    block = ((rows * bins // 128 + 8, 128) if cube else (half, bins + 128), f32)
    carried = []
    for p in range(PIECES):
        final = p == PIECES - 1
        ins = [spectrum, h, *numers[0], *numers[p], *wt, *carried]
        outs = [
            ((half, frames), f32),
            ((half if final else atoms, bins), f32),
            ((atoms, 128), f32),
            ((bins, size), bf16),
            ((2 * atoms, size), bf16),
        ]
        fresh, *made = call(
            functools.partial(second_kernel, start=p * size, n_parts=len(wt), before=p > 0, n_out=n_out * final),
            ins + ([fresh] if p else []),
            outs + [block] * n_out * final,
            scratch=[
                ((atoms, size), f32),
                ((bins, size), bf16),
                ((atoms, 128), f32),
                ((half, bins), f32),
                pltpu.SemaphoreType.DMA((size // NC,)),
            ],
            in_specs=[WHOLE] * len(ins) + [HBM] if p else [],
            out_specs=[HBM],
            aliases={len(ins): 0} if p else None,
        )
        before, carried = carried[2:], made[:4]
    away = made[4:]
    home = call(third_kernel, carried + before, [block] * n_out, scratch=[((half, bins), f32)], flops=10**9)
    if cube:
        total = away[REDUCE_CROSS & 3]
        for s in (3, 2, 1):
            total = total + hop(away[s ^ (REDUCE_CROSS & 3)], s)
        more = hop(total, REDUCE_CROSS)
        total = home[0]
        for s in (3, 2, 1):
            total = total + hop(home[s], s)
        (new,) = call(last_kernel, [kept, total, more], [((rows, bins), f32)], mib=16)
        return fresh, new
    total = lax.psum_scatter(jnp.concatenate([*home, *away]), "frames", scatter_dimension=0, tiled=True)
    return fresh, atoms_by_bin * total[:, :bins] / total[:, bins : bins + 1]


def solution(mesh):
    return jax.shard_map(
        functools.partial(body, n_dev=mesh.shape["frames"]),
        mesh=mesh,
        in_specs=(P("bins", ("groups", "frames")), P("frames", ("groups", "bins")), P("bins", ("groups", "frames"))),
        out_specs=(P("bins", ("groups", "frames")), P("frames", ("groups", "bins"))),
        check_vma=False,
    )
```

```python
import functools

import jax
import jax.numpy as jnp
from jax import lax
from jax.experimental import pallas as pl
from jax.experimental.pallas import tpu as pltpu
from jax.sharding import PartitionSpec as P

f32, bf16 = jnp.float32, jnp.bfloat16
WHOLE = pl.BlockSpec(memory_space=pltpu.VMEM)
HBM = pl.BlockSpec(memory_space=pl.ANY)
GATHER_CROSS, REDUCE_CROSS = 4, 6
PIECES = 2
FC, NC = 256, 512


def split(x):
    hi = x.astype(bf16)
    return hi, (x - hi.astype(f32)).astype(bf16)


def dot(a, b):
    return jnp.dot(a, b, preferred_element_type=f32)


def dot_nt(a, b):
    return lax.dot_general(a, b, (((1,), (1,)), ((), ())), preferred_element_type=f32)


def rows_at(start, rows):
    return pl.ds(pl.multiple_of(start * rows, rows), rows)


def pack(columns, rows):
    lane = lax.broadcasted_iota(jnp.int32, (8, 128), 1) // (1024 // rows)
    tile = jnp.zeros((8, 128), f32)
    for i in range(rows // 8):
        tile = jnp.where(lane == i, columns(8 * i), tile)
    return tile


def unpack(tile, i, rows):
    lane = i * (1024 // rows)
    return jnp.broadcast_to(tile[:, lane : lane + 1], (8, 128))


def whereabouts(cube):
    place, core = lax.axis_index("frames"), lax.axis_index("bins")
    return (place & 3, core ^ (place >> 2)) if cube else (place, core)


def prepare(ws, w2, wt, mass, first, columns):
    rows = ws[0].shape[0]
    half = len(ws) * rows
    place_of_mine = whereabouts(True)[0]
    for s, w in enumerate(ws):
        x = w[:, columns]
        hi, lo = split(x)
        place = (place_of_mine ^ (s ^ first)) if len(ws) > 1 else 0
        w2[rows_at(place, rows), columns] = hi
        w2[rows_at(place + half // rows, rows), columns] = lo
        total = sum(x[:, i : i + 128] for i in range(0, x.shape[1], 128))
        if columns.start:
            total = total + mass[rows_at(place, rows), :]
        if columns.stop == w.shape[1]:
            total = jnp.broadcast_to(jnp.sum(total, axis=1, keepdims=True), total.shape)
        mass[rows_at(place, rows), :] = total
    wt[columns, :] = w2[:, columns].T


def prepare_kernel(*refs):
    *ws, w2, wt, mass = refs
    prepare(ws, w2, wt, mass, 0, slice(0, wt.shape[0]))


def own_kernel(hown, atoms, h, h2, kept, *, cube):
    place_rows(hown, h, h2, whereabouts(cube)[1])
    kept[...] = atoms[...]


def other_kernel(hoth, _h, _h2, h, h2, *, cube):
    place_rows(hoth, h, h2, 1 - whereabouts(cube)[1])


def place_rows(old, h, h2, place):
    half = old.shape[0]
    x = old[...]
    hi, lo = split(x)
    h[rows_at(place, half), :] = x
    h2[rows_at(place, half), :] = hi
    h2[rows_at(place + 2, half), :] = lo


def hi_lo(parts, rows):
    half = parts[0].shape[1] // 2
    return [w[rows, :half] for w in parts], [w[rows, half:] for w in parts]


def by_three(parts, rows):
    hi, lo = hi_lo(parts, rows)
    return jnp.concatenate(hi + lo + hi, axis=1)


def near_kernel(wt, h2, model):
    half = wt.shape[1] // 2
    h = jnp.concatenate([h2[:half, :], h2[:half, :]], axis=0)
    for f in range(0, wt.shape[0], FC):
        model[f : f + FC, :] = dot(wt[f : f + FC, :], h)


def first_kernel(v, h2, *refs, start, n_parts, masses, raw, near):
    refs = list(refs)
    take = lambda n: [refs.pop(0) for _ in range(n)]
    (model,) = take(1) if near else (None,)
    w2, wt = take(n_parts), take(n_parts)
    mass, ws, (numer,) = take(masses), take(raw), take(1)
    if raw:
        made = take(3)
        w2.append(made[0])
        wt.append(made[1])
        mass.append(made[2])
    rhi, rlo = refs
    bins, frames = rhi.shape
    atoms = h2.shape[0] // 2
    for n in range(0, frames, NC):
        at, src = slice(n, n + NC), slice(start + n, start + n + NC)
        top = h2[atoms // 2 if near else 0 : atoms, src]
        h3 = jnp.concatenate([top, top, h2[atoms:, src]], axis=0)
        for f in range(0, bins, FC):
            rows = slice(f, f + FC)
            if raw and n == 0:
                prepare(ws, *made, GATHER_CROSS & 3, rows)
            if near:
                hi, lo = hi_lo(wt, rows)
                m = model[rows, src] + dot(jnp.concatenate([hi[1], lo[1], *hi], axis=1), h3)
            else:
                m = dot(by_three(wt, rows), h3)
            hi, lo = split(v[rows, src] / m)
            rhi[rows, at] = hi
            rlo[rows, at] = lo
        whi = jnp.concatenate([w[: w.shape[0] // 2, :] for w in w2], axis=0)
        wlo = jnp.concatenate([w[w.shape[0] // 2 :, :] for w in w2], axis=0)
        numer[:atoms, at] = dot(whi, rhi[:, at]) + dot(wlo, rhi[:, at]) + dot(whi, rlo[:, at])
    if mass:
        part = mass[0].shape[0]
        numer[atoms:, :] = jnp.zeros((8, frames), f32)
        numer[atoms:, :128] = pack(lambda i: mass[i // part][i % part : i % part + 8, :], atoms)


def second_kernel(v, h, mine, theirs, nown, noth, *refs, start, n_parts, before, n_out):
    refs = list(refs)
    take = lambda n: [refs.pop(0) for _ in range(n)]
    wt = take(n_parts)
    if before:
        acc_in, row_in, other_rhi, other_f2, _ = take(5)
    newact, acc, row_mass, rhi, f2 = take(5)
    outs = take(n_out)
    fresh, rlo, scale, cross, o_sems = refs
    bins, frames = rhi.shape
    atoms = h.shape[0]
    half = atoms // 2
    half_of_mine = whereabouts(n_parts > 1)[1]
    tile = 1.0 / (mine[atoms:, :128] + theirs[atoms:, :128])
    for i in range(atoms // 8):
        scale[8 * i : 8 * i + 8, :] = unpack(tile, i, atoms)
    sums = row_in[:, :1] if before else None
    written = []
    for n in range(0, frames, NC):
        at, src = slice(n, n + NC), slice(start + n, start + n + NC)
        x = h[:, src] * (nown[:atoms, at] + noth[:atoms, at]) * scale[:, :1]
        fresh[:, at] = x
        hi, lo = split(x)
        f2[:atoms, at] = hi
        f2[atoms:, at] = lo
        row = jnp.sum(x, axis=1, keepdims=True)
        sums = row if sums is None else sums + row
        written.append(
            pltpu.make_async_copy(
                fresh.at[rows_at(half_of_mine, half), pl.ds(n, NC)],
                newact.at[:, pl.ds(start + n, NC)],
                o_sems.at[n // NC],
            )
        )
        written[-1].start()
        h3 = jnp.concatenate([f2[:atoms, at], f2[:atoms, at], f2[atoms:, at]], axis=0)
        for f in range(0, bins, FC):
            m = dot(by_three(wt, slice(f, f + FC)), h3)
            hi, lo = split(v[f : f + FC, src] / m)
            rhi[f : f + FC, at] = hi
            rlo[f : f + FC, at] = lo
    row_mass[...] = jnp.broadcast_to(sums, (atoms, 128))
    total = dot_nt(f2[:atoms, :], rlo[...])
    if before:
        total = total + acc_in[...]
        acc[...] = total[:half, :]
        cross[...] = total[half:, :] + by_high(half, (f2, rhi), (other_f2, other_rhi))
        write_blocks(outs, cross, row_mass, half, atoms // 8)
    else:
        acc[...] = total
    for copy in written:
        copy.wait()


def by_high(start, *pairs):
    total = None
    for f2, rhi in pairs:
        atoms = f2.shape[0] // 2
        half = atoms // 2
        rows = [f2[start : start + half, :], f2[atoms + start : atoms + start + half, :]]
        x = dot_nt(jnp.concatenate(rows, axis=0), rhi[...])
        total = x if total is None else total + x
    return total[: total.shape[0] // 2, :] + total[total.shape[0] // 2 :, :]


def write_blocks(outs, acc, row_mass, start, rows):
    bins = acc.shape[1]
    if len(outs) == 1:
        outs[0][:, :bins] = acc[...]
        outs[0][:, bins:] = row_mass[start : start + acc.shape[0], :]
        return
    place_of_mine = whereabouts(True)[0]
    for s, o in enumerate(outs):
        base = pl.multiple_of((place_of_mine ^ s) * rows, rows)
        for i in range(rows // 8):
            for j in range(bins // 128):
                k = 8 * (i * (bins // 128) + j)
                o[k : k + 8, :] = acc[pl.ds(base + 8 * i, 8), 128 * j : 128 * (j + 1)]
        o[rows * bins // 128 :, :] = pack(lambda i: row_mass[pl.ds(start + base + i, 8), :], rows)


def third_kernel(acc, row_mass, rhi_a, f2_a, rhi_b, f2_b, *refs):
    *outs, own = refs
    own[...] = acc[...] + by_high(0, (f2_b, rhi_b), (f2_a, rhi_a))
    write_blocks(outs, own, row_mass, 0, f2_a.shape[0] // 16)


def last_kernel(old, total, more, new):
    rows, bins = old.shape
    x = 1.0 / (total[rows * bins // 128 :, :] + more[rows * bins // 128 :, :])
    for i in range(rows // 8):
        scale = unpack(x, i, rows)
        for j in range(bins // 128):
            k = 8 * (i * (bins // 128) + j)
            at = (slice(8 * i, 8 * i + 8), slice(128 * j, 128 * (j + 1)))
            new[at] = old[at] * (total[k : k + 8, :] + more[k : k + 8, :]) * scale


def call(kernel, ins, outs, scratch=(), in_specs=(), out_specs=(), aliases=None, mib=28, flops=0):
    return pl.pallas_call(
        kernel,
        in_specs=list(in_specs) + [WHOLE] * (len(ins) - len(in_specs)),
        out_specs=list(out_specs) + [WHOLE] * (len(outs) - len(out_specs)),
        out_shape=[jax.ShapeDtypeStruct(*o) for o in outs],
        scratch_shapes=[pltpu.VMEM(*s) if isinstance(s, tuple) else s for s in scratch],
        input_output_aliases=aliases or {},
        compiler_params=pltpu.CompilerParams(vmem_limit_bytes=mib * 2**20),
        cost_estimate=pl.CostEstimate(flops=flops, bytes_accessed=0, transcendentals=0) if flops else None,
    )(*ins)


def hop(x, step):
    return lax.ppermute(x, "frames", [(i, i ^ step) for i in range(8)])


def body(spectrum, atoms_by_bin, activations, *, n_dev):
    swap = lambda x: lax.ppermute(x, "bins", [(0, 1), (1, 0)])
    bins, frames = spectrum.shape
    half = activations.shape[0]
    atoms = 2 * half
    rows = atoms_by_bin.shape[0]
    cube = n_dev == 8 and rows % 16 == 0
    size = frames // PIECES

    def basis_outs(k):
        return [((2 * k, bins), bf16), ((bins, 2 * k), bf16), ((k, 128), f32)]

    ordered = [((atoms, frames), f32), ((2 * atoms, frames), bf16)]
    h, h2, kept = call(
        functools.partial(own_kernel, cube=cube),
        [activations, atoms_by_bin],
        ordered + [((rows, bins), f32)],
        mib=16,
        flops=10**10,
    )
    raw = []
    if cube:
        near = [hop(atoms_by_bin, s) for s in (1, 2, 3)]
        far = hop(atoms_by_bin, GATHER_CROSS)
        raw = [far] + [hop(far, s) for s in (1, 2, 3)]
        near = [kept, *near]
    else:
        near = [lax.all_gather(atoms_by_bin, "frames", axis=0, tiled=True)]
    h, h2 = call(
        functools.partial(other_kernel, cube=cube),
        [swap(activations), h, h2],
        ordered,
        aliases={1: 0, 2: 1},
        mib=16,
        flops=10**9,
    )
    k = sum(w.shape[0] for w in near)
    w2, wt, mass = call(prepare_kernel, near, basis_outs(k), mib=16, flops=10**10)
    model = call(near_kernel, [wt, h2], [((bins, frames), f32)], mib=16, flops=10**10) if cube else []
    w2, wt, mass = [w2], [wt], [mass]
    numers = []
    for p in range(PIECES):
        numer, *made = call(
            functools.partial(first_kernel, start=p * size, n_parts=len(wt), masses=len(mass), raw=len(raw), near=cube),
            [spectrum, h2, *model, *w2, *wt, *mass, *raw],
            [((atoms + 8 * (p == 0), size), f32)] + (basis_outs(atoms - k) if raw else []),
            scratch=[((bins, size), bf16), ((bins, size), bf16)],
        )
        if raw:
            w2.append(made[0])
            wt.append(made[1])
        raw, mass = [], []
        numers.append((numer, swap(numer)))
    n_out = 4 if cube else 1
    block = ((rows * bins // 128 + 8, 128) if cube else (half, bins + 128), f32)
    carried = []
    for p in range(PIECES):
        final = p == PIECES - 1
        ins = [spectrum, h, *numers[0], *numers[p], *wt, *carried]
        outs = [
            ((half, frames), f32),
            ((half if final else atoms, bins), f32),
            ((atoms, 128), f32),
            ((bins, size), bf16),
            ((2 * atoms, size), bf16),
        ]
        fresh, *made = call(
            functools.partial(second_kernel, start=p * size, n_parts=len(wt), before=p > 0, n_out=n_out * final),
            ins + ([fresh] if p else []),
            outs + [block] * n_out * final,
            scratch=[
                ((atoms, size), f32),
                ((bins, size), bf16),
                ((atoms, 128), f32),
                ((half, bins), f32),
                pltpu.SemaphoreType.DMA((size // NC,)),
            ],
            in_specs=[WHOLE] * len(ins) + [HBM] if p else [],
            out_specs=[HBM],
            aliases={len(ins): 0} if p else None,
        )
        before, carried = carried[2:], made[:4]
    away = made[4:]
    home = call(third_kernel, carried + before, [block] * n_out, scratch=[((half, bins), f32)], flops=10**9)
    if cube:
        total = away[REDUCE_CROSS & 3]
        for s in (2, 1, 3):
            total = total + hop(away[s ^ (REDUCE_CROSS & 3)], s)
        more = hop(total, REDUCE_CROSS)
        total = home[0]
        for s in (1, 3, 2):
            total = total + hop(home[s], s)
        (new,) = call(last_kernel, [kept, total, more], [((rows, bins), f32)], mib=16)
        return fresh, new
    total = lax.psum_scatter(jnp.concatenate([*home, *away]), "frames", scatter_dimension=0, tiled=True)
    return fresh, atoms_by_bin * total[:, :bins] / total[:, bins : bins + 1]


def solution(mesh):
    return jax.shard_map(
        functools.partial(body, n_dev=mesh.shape["frames"]),
        mesh=mesh,
        in_specs=(P("bins", ("groups", "frames")), P("frames", ("groups", "bins")), P("bins", ("groups", "frames"))),
        out_specs=(P("bins", ("groups", "frames")), P("frames", ("groups", "bins"))),
        check_vma=False,
    )
```

```python
import functools

import jax
import jax.numpy as jnp
from jax import lax
from jax.experimental import pallas as pl
from jax.experimental.pallas import tpu as pltpu
from jax.sharding import PartitionSpec as P

f32, bf16 = jnp.float32, jnp.bfloat16
WHOLE = pl.BlockSpec(memory_space=pltpu.VMEM)
HBM = pl.BlockSpec(memory_space=pl.ANY)
GATHER_CROSS, REDUCE_CROSS = 4, 6
PIECES = 2
FC, FIRST_FC, NC = 256, 128, 512


def split(x):
    hi = x.astype(bf16)
    return hi, (x - hi.astype(f32)).astype(bf16)


def dot(a, b):
    return jnp.dot(a, b, preferred_element_type=f32)


def dot_nt(a, b):
    return lax.dot_general(a, b, (((1,), (1,)), ((), ())), preferred_element_type=f32)


def rows_at(start, rows):
    return pl.ds(pl.multiple_of(start * rows, rows), rows)


def pack(columns, rows):
    lane = lax.broadcasted_iota(jnp.int32, (8, 128), 1) // (1024 // rows)
    tile = jnp.zeros((8, 128), f32)
    for i in range(rows // 8):
        tile = jnp.where(lane == i, columns(8 * i), tile)
    return tile


def unpack(tile, i, rows):
    lane = i * (1024 // rows)
    return jnp.broadcast_to(tile[:, lane : lane + 1], (8, 128))


def whereabouts(cube):
    place, core = lax.axis_index("frames"), lax.axis_index("bins")
    return (place & 3, core ^ (place >> 2)) if cube else (place, core)


def prepare(ws, w2, wt, mass, first, columns):
    rows = ws[0].shape[0]
    half = len(ws) * rows
    place_of_mine = whereabouts(True)[0]
    for s, w in enumerate(ws):
        x = w[:, columns]
        hi, lo = split(x)
        place = (place_of_mine ^ (s ^ first)) if len(ws) > 1 else 0
        w2[rows_at(place, rows), columns] = hi
        w2[rows_at(place + half // rows, rows), columns] = lo
        total = sum(x[:, i : i + 128] for i in range(0, x.shape[1], 128))
        if columns.start:
            total = total + mass[rows_at(place, rows), :]
        if columns.stop == w.shape[1]:
            total = jnp.broadcast_to(jnp.sum(total, axis=1, keepdims=True), total.shape)
        mass[rows_at(place, rows), :] = total
    wt[columns, :] = w2[:, columns].T


def prepare_kernel(*refs):
    *ws, w2, wt, mass = refs
    prepare(ws, w2, wt, mass, 0, slice(0, wt.shape[0]))


def own_kernel(hown, atoms, h, h2, kept, *, cube):
    place_rows(hown, h, h2, whereabouts(cube)[1])
    kept[...] = atoms[...]


def other_kernel(hoth, _h, _h2, h, h2, *, cube):
    place_rows(hoth, h, h2, 1 - whereabouts(cube)[1])


def place_rows(old, h, h2, place):
    half = old.shape[0]
    x = old[...]
    hi, lo = split(x)
    h[rows_at(place, half), :] = x
    h2[rows_at(place, half), :] = hi
    h2[rows_at(place + 2, half), :] = lo


def hi_lo(parts, rows):
    half = parts[0].shape[1] // 2
    return [w[rows, :half] for w in parts], [w[rows, half:] for w in parts]


def by_three(parts, rows):
    hi, lo = hi_lo(parts, rows)
    return jnp.concatenate(hi + lo + hi, axis=1)


def near_kernel(wt, h2, model):
    half = wt.shape[1] // 2
    h = jnp.concatenate([h2[:half, :], h2[:half, :]], axis=0)
    for f in range(0, wt.shape[0], FC):
        model[f : f + FC, :] = dot(wt[f : f + FC, :], h)


def first_kernel(v, h2, *refs, start, n_parts, masses, raw, near):
    refs = list(refs)
    take = lambda n: [refs.pop(0) for _ in range(n)]
    (model,) = take(1) if near else (None,)
    w2, wt = take(n_parts), take(n_parts)
    mass, ws, (numer,) = take(masses), take(raw), take(1)
    if raw:
        made = take(3)
        w2.append(made[0])
        wt.append(made[1])
        mass.append(made[2])
    rhi, rlo = refs
    bins, frames = rhi.shape
    atoms = h2.shape[0] // 2
    for n in range(0, frames, NC):
        at, src = slice(n, n + NC), slice(start + n, start + n + NC)
        top = h2[atoms // 2 if near else 0 : atoms, src]
        h3 = jnp.concatenate([top, top, h2[atoms:, src]], axis=0)
        for f in range(0, bins, FIRST_FC):
            rows = slice(f, f + FIRST_FC)
            if raw and n == 0:
                prepare(ws, *made, GATHER_CROSS & 3, rows)
            if near:
                hi, lo = hi_lo(wt, rows)
                m = model[rows, src] + dot(jnp.concatenate([hi[1], lo[1], *hi], axis=1), h3)
            else:
                m = dot(by_three(wt, rows), h3)
            hi, lo = split(v[rows, src] / m)
            rhi[rows, at] = hi
            rlo[rows, at] = lo
        whi = jnp.concatenate([w[: w.shape[0] // 2, :] for w in w2], axis=0)
        wlo = jnp.concatenate([w[w.shape[0] // 2 :, :] for w in w2], axis=0)
        numer[:atoms, at] = dot(whi, rhi[:, at]) + dot(wlo, rhi[:, at]) + dot(whi, rlo[:, at])
    if mass:
        part = mass[0].shape[0]
        numer[atoms:, :] = jnp.zeros((8, frames), f32)
        numer[atoms:, :128] = pack(lambda i: mass[i // part][i % part : i % part + 8, :], atoms)


def second_kernel(v, h, mine, theirs, nown, noth, *refs, start, n_parts, before, n_out):
    refs = list(refs)
    take = lambda n: [refs.pop(0) for _ in range(n)]
    wt = take(n_parts)
    if before:
        acc_in, row_in, other_rhi, other_f2, _ = take(5)
    newact, acc, row_mass, rhi, f2 = take(5)
    outs = take(n_out)
    fresh, rlo, scale, cross, o_sems = refs
    bins, frames = rhi.shape
    atoms = h.shape[0]
    half = atoms // 2
    half_of_mine = whereabouts(n_parts > 1)[1]
    tile = 1.0 / (mine[atoms:, :128] + theirs[atoms:, :128])
    for i in range(atoms // 8):
        scale[8 * i : 8 * i + 8, :] = unpack(tile, i, atoms)
    sums = row_in[:, :1] if before else None
    written = []
    for n in range(0, frames, NC):
        at, src = slice(n, n + NC), slice(start + n, start + n + NC)
        x = h[:, src] * (nown[:atoms, at] + noth[:atoms, at]) * scale[:, :1]
        fresh[:, at] = x
        hi, lo = split(x)
        f2[:atoms, at] = hi
        f2[atoms:, at] = lo
        row = jnp.sum(x, axis=1, keepdims=True)
        sums = row if sums is None else sums + row
        written.append(
            pltpu.make_async_copy(
                fresh.at[rows_at(half_of_mine, half), pl.ds(n, NC)],
                newact.at[:, pl.ds(start + n, NC)],
                o_sems.at[n // NC],
            )
        )
        written[-1].start()
        h3 = jnp.concatenate([f2[:atoms, at], f2[:atoms, at], f2[atoms:, at]], axis=0)
        for f in range(0, bins, FC):
            m = dot(by_three(wt, slice(f, f + FC)), h3)
            hi, lo = split(v[f : f + FC, src] / m)
            rhi[f : f + FC, at] = hi
            rlo[f : f + FC, at] = lo
    row_mass[...] = jnp.broadcast_to(sums, (atoms, 128))
    total = dot_nt(f2[:atoms, :], rlo[...])
    if before:
        total = total + acc_in[...]
        acc[...] = total[:half, :]
        cross[...] = total[half:, :] + by_high(half, (f2, rhi), (other_f2, other_rhi))
        write_blocks(outs, cross, row_mass, half, atoms // 8)
    else:
        acc[...] = total
    for copy in written:
        copy.wait()


def by_high(start, *pairs):
    total = None
    for f2, rhi in pairs:
        atoms = f2.shape[0] // 2
        half = atoms // 2
        rows = [f2[start : start + half, :], f2[atoms + start : atoms + start + half, :]]
        x = dot_nt(jnp.concatenate(rows, axis=0), rhi[...])
        total = x if total is None else total + x
    return total[: total.shape[0] // 2, :] + total[total.shape[0] // 2 :, :]


def write_blocks(outs, acc, row_mass, start, rows):
    bins = acc.shape[1]
    if len(outs) == 1:
        outs[0][:, :bins] = acc[...]
        outs[0][:, bins:] = row_mass[start : start + acc.shape[0], :]
        return
    place_of_mine = whereabouts(True)[0]
    for s, o in enumerate(outs):
        base = pl.multiple_of((place_of_mine ^ s) * rows, rows)
        for i in range(rows // 8):
            for j in range(bins // 128):
                k = 8 * (i * (bins // 128) + j)
                o[k : k + 8, :] = acc[pl.ds(base + 8 * i, 8), 128 * j : 128 * (j + 1)]
        o[rows * bins // 128 :, :] = pack(lambda i: row_mass[pl.ds(start + base + i, 8), :], rows)


def third_kernel(acc, row_mass, rhi_a, f2_a, rhi_b, f2_b, *refs):
    *outs, own = refs
    own[...] = acc[...] + by_high(0, (f2_b, rhi_b), (f2_a, rhi_a))
    write_blocks(outs, own, row_mass, 0, f2_a.shape[0] // 16)


def last_kernel(old, total, more, new):
    rows, bins = old.shape
    x = 1.0 / (total[rows * bins // 128 :, :] + more[rows * bins // 128 :, :])
    for i in range(rows // 8):
        scale = unpack(x, i, rows)
        for j in range(bins // 128):
            k = 8 * (i * (bins // 128) + j)
            at = (slice(8 * i, 8 * i + 8), slice(128 * j, 128 * (j + 1)))
            new[at] = old[at] * (total[k : k + 8, :] + more[k : k + 8, :]) * scale


def call(kernel, ins, outs, scratch=(), in_specs=(), out_specs=(), aliases=None, mib=28, flops=0):
    return pl.pallas_call(
        kernel,
        in_specs=list(in_specs) + [WHOLE] * (len(ins) - len(in_specs)),
        out_specs=list(out_specs) + [WHOLE] * (len(outs) - len(out_specs)),
        out_shape=[jax.ShapeDtypeStruct(*o) for o in outs],
        scratch_shapes=[pltpu.VMEM(*s) if isinstance(s, tuple) else s for s in scratch],
        input_output_aliases=aliases or {},
        compiler_params=pltpu.CompilerParams(vmem_limit_bytes=mib * 2**20),
        cost_estimate=pl.CostEstimate(flops=flops, bytes_accessed=0, transcendentals=0) if flops else None,
    )(*ins)


def hop(x, step):
    return lax.ppermute(x, "frames", [(i, i ^ step) for i in range(8)])


def body(spectrum, atoms_by_bin, activations, *, n_dev):
    swap = lambda x: lax.ppermute(x, "bins", [(0, 1), (1, 0)])
    bins, frames = spectrum.shape
    half = activations.shape[0]
    atoms = 2 * half
    rows = atoms_by_bin.shape[0]
    cube = n_dev == 8 and rows % 16 == 0
    size = frames // PIECES

    def basis_outs(k):
        return [((2 * k, bins), bf16), ((bins, 2 * k), bf16), ((k, 128), f32)]

    ordered = [((atoms, frames), f32), ((2 * atoms, frames), bf16)]
    h, h2, kept = call(
        functools.partial(own_kernel, cube=cube),
        [activations, atoms_by_bin],
        ordered + [((rows, bins), f32)],
        mib=16,
        flops=10**10,
    )
    raw = []
    if cube:
        near = [hop(atoms_by_bin, s) for s in (1, 2, 3)]
        far = hop(atoms_by_bin, GATHER_CROSS)
        raw = [far] + [hop(far, s) for s in (1, 2, 3)]
        near = [kept, *near]
    else:
        near = [lax.all_gather(atoms_by_bin, "frames", axis=0, tiled=True)]
    h, h2 = call(
        functools.partial(other_kernel, cube=cube),
        [swap(activations), h, h2],
        ordered,
        aliases={1: 0, 2: 1},
        mib=16,
        flops=10**9,
    )
    k = sum(w.shape[0] for w in near)
    w2, wt, mass = call(prepare_kernel, near, basis_outs(k), mib=16, flops=10**10)
    model = call(near_kernel, [wt, h2], [((bins, frames), f32)], mib=16, flops=10**9) if cube else []
    w2, wt, mass = [w2], [wt], [mass]
    numers = []
    for p in range(PIECES):
        numer, *made = call(
            functools.partial(first_kernel, start=p * size, n_parts=len(wt), masses=len(mass), raw=len(raw), near=cube),
            [spectrum, h2, *model, *w2, *wt, *mass, *raw],
            [((atoms + 8 * (p == 0), size), f32)] + (basis_outs(atoms - k) if raw else []),
            scratch=[((bins, size), bf16), ((bins, size), bf16)],
        )
        if raw:
            w2.append(made[0])
            wt.append(made[1])
        raw, mass = [], []
        numers.append((numer, swap(numer)))
    n_out = 4 if cube else 1
    block = ((rows * bins // 128 + 8, 128) if cube else (half, bins + 128), f32)
    carried = []
    for p in range(PIECES):
        final = p == PIECES - 1
        ins = [spectrum, h, *numers[0], *numers[p], *wt, *carried]
        outs = [
            ((half, frames), f32),
            ((half if final else atoms, bins), f32),
            ((atoms, 128), f32),
            ((bins, size), bf16),
            ((2 * atoms, size), bf16),
        ]
        fresh, *made = call(
            functools.partial(second_kernel, start=p * size, n_parts=len(wt), before=p > 0, n_out=n_out * final),
            ins + ([fresh] if p else []),
            outs + [block] * n_out * final,
            scratch=[
                ((atoms, size), f32),
                ((bins, size), bf16),
                ((atoms, 128), f32),
                ((half, bins), f32),
                pltpu.SemaphoreType.DMA((size // NC,)),
            ],
            in_specs=[WHOLE] * len(ins) + [HBM] if p else [],
            out_specs=[HBM],
            aliases={len(ins): 0} if p else None,
        )
        before, carried = carried[2:], made[:4]
    away = made[4:]
    home = call(third_kernel, carried + before, [block] * n_out, scratch=[((half, bins), f32)], flops=10**9)
    if cube:
        total = away[REDUCE_CROSS & 3]
        for s in (2, 1, 3):
            total = total + hop(away[s ^ (REDUCE_CROSS & 3)], s)
        more = hop(total, REDUCE_CROSS)
        total = home[0]
        for s in (1, 3, 2):
            total = total + hop(home[s], s)
        (new,) = call(last_kernel, [kept, total, more], [((rows, bins), f32)], mib=16)
        return fresh, new
    total = lax.psum_scatter(jnp.concatenate([*home, *away]), "frames", scatter_dimension=0, tiled=True)
    return fresh, atoms_by_bin * total[:, :bins] / total[:, bins : bins + 1]


def solution(mesh):
    return jax.shard_map(
        functools.partial(body, n_dev=mesh.shape["frames"]),
        mesh=mesh,
        in_specs=(P("bins", ("groups", "frames")), P("frames", ("groups", "bins")), P("bins", ("groups", "frames"))),
        out_specs=(P("bins", ("groups", "frames")), P("frames", ("groups", "bins"))),
        check_vma=False,
    )
```

```python
import functools

import jax
import jax.numpy as jnp
from jax import lax
from jax.experimental import pallas as pl
from jax.experimental.pallas import tpu as pltpu
from jax.sharding import PartitionSpec as P

f32, bf16 = jnp.float32, jnp.bfloat16
WHOLE = pl.BlockSpec(memory_space=pltpu.VMEM)
HBM = pl.BlockSpec(memory_space=pl.ANY)
GATHER_CROSS, REDUCE_CROSS = 4, 6
PIECES = 2
FC, FIRST_FC, NC = 256, 128, 512


def split(x):
    hi = x.astype(bf16)
    return hi, (x - hi.astype(f32)).astype(bf16)


def dot(a, b):
    return jnp.dot(a, b, preferred_element_type=f32)


def dot_nt(a, b):
    return lax.dot_general(a, b, (((1,), (1,)), ((), ())), preferred_element_type=f32)


def rows_at(start, rows):
    return pl.ds(pl.multiple_of(start * rows, rows), rows)


def pack(columns, rows):
    lane = lax.broadcasted_iota(jnp.int32, (8, 128), 1) // (1024 // rows)
    tile = jnp.zeros((8, 128), f32)
    for i in range(rows // 8):
        tile = jnp.where(lane == i, columns(8 * i), tile)
    return tile


def unpack(tile, i, rows):
    lane = i * (1024 // rows)
    return jnp.broadcast_to(tile[:, lane : lane + 1], (8, 128))


def whereabouts(cube):
    place, core = lax.axis_index("frames"), lax.axis_index("bins")
    return (place & 3, core ^ (place >> 2)) if cube else (place, core)


def prepare(ws, w2, wt, mass, first, columns):
    rows = ws[0].shape[0]
    half = len(ws) * rows
    place_of_mine = whereabouts(True)[0]
    for s, w in enumerate(ws):
        x = w[:, columns]
        hi, lo = split(x)
        place = (place_of_mine ^ (s ^ first)) if len(ws) > 1 else 0
        w2[rows_at(place, rows), columns] = hi
        w2[rows_at(place + half // rows, rows), columns] = lo
        total = sum(x[:, i : i + 128] for i in range(0, x.shape[1], 128))
        if columns.start:
            total = total + mass[rows_at(place, rows), :]
        if columns.stop == w.shape[1]:
            total = jnp.broadcast_to(jnp.sum(total, axis=1, keepdims=True), total.shape)
        mass[rows_at(place, rows), :] = total
    wt[columns, :] = w2[:, columns].T


def prepare_kernel(*refs):
    *ws, w2, wt, mass = refs
    prepare(ws, w2, wt, mass, 0, slice(0, wt.shape[0]))


def own_kernel(hown, atoms, h, h2, kept, *, cube):
    place_rows(hown, h, h2, whereabouts(cube)[1])
    kept[...] = atoms[...]


def other_kernel(hoth, _h, _h2, h, h2, *, cube):
    place_rows(hoth, h, h2, 1 - whereabouts(cube)[1])


def place_rows(old, h, h2, place):
    half = old.shape[0]
    x = old[...]
    hi, lo = split(x)
    h[rows_at(place, half), :] = x
    h2[rows_at(place, half), :] = hi
    h2[rows_at(place + 2, half), :] = lo


def hi_lo(parts, rows):
    half = parts[0].shape[1] // 2
    return [w[rows, :half] for w in parts], [w[rows, half:] for w in parts]


def by_three(parts, rows):
    hi, lo = hi_lo(parts, rows)
    return jnp.concatenate(hi + lo + hi, axis=1)


def near_kernel(wt, h2, model):
    half = wt.shape[1] // 2
    h = jnp.concatenate([h2[:half, :], h2[:half, :]], axis=0)
    for f in range(0, wt.shape[0], FC):
        model[f : f + FC, :] = dot(wt[f : f + FC, :], h)


def first_kernel(v, h2, *refs, start, n_parts, masses, raw, near):
    refs = list(refs)
    take = lambda n: [refs.pop(0) for _ in range(n)]
    (model,) = take(1) if near else (None,)
    w2, wt = take(n_parts), take(n_parts)
    mass, ws, (numer,) = take(masses), take(raw), take(1)
    if raw:
        made = take(3)
        w2.append(made[0])
        wt.append(made[1])
        mass.append(made[2])
    rhi, rlo = refs
    bins, frames = rhi.shape
    atoms = h2.shape[0] // 2
    for n in range(0, frames, NC):
        at, src = slice(n, n + NC), slice(start + n, start + n + NC)
        top = h2[atoms // 2 if near else 0 : atoms, src]
        h3 = jnp.concatenate([top, top, h2[atoms:, src]], axis=0)
        for f in range(0, bins, FIRST_FC):
            rows = slice(f, f + FIRST_FC)
            if raw and n == 0:
                prepare(ws, *made, GATHER_CROSS & 3, rows)
            if near:
                hi, lo = hi_lo(wt, rows)
                m = model[rows, src] + dot(jnp.concatenate([hi[1], lo[1], *hi], axis=1), h3)
            else:
                m = dot(by_three(wt, rows), h3)
            hi, lo = split(v[rows, src] / m)
            rhi[rows, at] = hi
            rlo[rows, at] = lo
        whi = jnp.concatenate([w[: w.shape[0] // 2, :] for w in w2], axis=0)
        both = dot(jnp.concatenate([w[...] for w in w2], axis=0), rhi[:, at])
        low = dot(whi, rlo[:, at])
        part = atoms // len(w2)
        for p in range(len(w2)):
            hi_rows = slice(2 * p * part, (2 * p + 1) * part)
            lo_rows = slice((2 * p + 1) * part, (2 * p + 2) * part)
            rows = slice(p * part, (p + 1) * part)
            numer[rows, at] = both[hi_rows, :] + both[lo_rows, :] + low[rows, :]
    if mass:
        part = mass[0].shape[0]
        numer[atoms:, :] = jnp.zeros((8, frames), f32)
        numer[atoms:, :128] = pack(lambda i: mass[i // part][i % part : i % part + 8, :], atoms)


def second_kernel(v, h, mine, theirs, nown, noth, *refs, start, n_parts, before, n_out):
    refs = list(refs)
    take = lambda n: [refs.pop(0) for _ in range(n)]
    wt = take(n_parts)
    if before:
        acc_in, row_in, other_rhi, other_f2, _ = take(5)
    newact, acc, row_mass, rhi, f2 = take(5)
    outs = take(n_out)
    fresh, rlo, scale, cross, o_sems = refs
    bins, frames = rhi.shape
    atoms = h.shape[0]
    half = atoms // 2
    half_of_mine = whereabouts(n_parts > 1)[1]
    tile = 1.0 / (mine[atoms:, :128] + theirs[atoms:, :128])
    for i in range(atoms // 8):
        scale[8 * i : 8 * i + 8, :] = unpack(tile, i, atoms)
    sums = row_in[:, :1] if before else None
    written = []
    for n in range(0, frames, NC):
        at, src = slice(n, n + NC), slice(start + n, start + n + NC)
        x = h[:, src] * (nown[:atoms, at] + noth[:atoms, at]) * scale[:, :1]
        fresh[:, at] = x
        hi, lo = split(x)
        f2[:atoms, at] = hi
        f2[atoms:, at] = lo
        row = jnp.sum(x, axis=1, keepdims=True)
        sums = row if sums is None else sums + row
        written.append(
            pltpu.make_async_copy(
                fresh.at[rows_at(half_of_mine, half), pl.ds(n, NC)],
                newact.at[:, pl.ds(start + n, NC)],
                o_sems.at[n // NC],
            )
        )
        written[-1].start()
        h3 = jnp.concatenate([f2[:atoms, at], f2[:atoms, at], f2[atoms:, at]], axis=0)
        for f in range(0, bins, FC):
            m = dot(by_three(wt, slice(f, f + FC)), h3)
            hi, lo = split(v[f : f + FC, src] / m)
            rhi[f : f + FC, at] = hi
            rlo[f : f + FC, at] = lo
    row_mass[...] = jnp.broadcast_to(sums, (atoms, 128))
    total = dot_nt(f2[:atoms, :], rlo[...])
    if before:
        total = total + acc_in[...]
        acc[...] = total[:half, :]
        cross[...] = total[half:, :] + by_high(half, (f2, rhi), (other_f2, other_rhi))
        write_blocks(outs, cross, row_mass, half, atoms // 8)
    else:
        acc[...] = total
    for copy in written:
        copy.wait()


def by_high(start, *pairs):
    total = None
    for f2, rhi in pairs:
        atoms = f2.shape[0] // 2
        half = atoms // 2
        rows = [f2[start : start + half, :], f2[atoms + start : atoms + start + half, :]]
        x = dot_nt(jnp.concatenate(rows, axis=0), rhi[...])
        total = x if total is None else total + x
    return total[: total.shape[0] // 2, :] + total[total.shape[0] // 2 :, :]


def write_blocks(outs, acc, row_mass, start, rows):
    bins = acc.shape[1]
    if len(outs) == 1:
        outs[0][:, :bins] = acc[...]
        outs[0][:, bins:] = row_mass[start : start + acc.shape[0], :]
        return
    place_of_mine = whereabouts(True)[0]
    for s, o in enumerate(outs):
        base = pl.multiple_of((place_of_mine ^ s) * rows, rows)
        for i in range(rows // 8):
            for j in range(bins // 128):
                k = 8 * (i * (bins // 128) + j)
                o[k : k + 8, :] = acc[pl.ds(base + 8 * i, 8), 128 * j : 128 * (j + 1)]
        o[rows * bins // 128 :, :] = pack(lambda i: row_mass[pl.ds(start + base + i, 8), :], rows)


def third_kernel(acc, row_mass, rhi_a, f2_a, rhi_b, f2_b, *refs):
    *outs, own = refs
    own[...] = acc[...] + by_high(0, (f2_b, rhi_b), (f2_a, rhi_a))
    write_blocks(outs, own, row_mass, 0, f2_a.shape[0] // 16)


def last_kernel(old, total, more, new):
    rows, bins = old.shape
    x = 1.0 / (total[rows * bins // 128 :, :] + more[rows * bins // 128 :, :])
    for i in range(rows // 8):
        scale = unpack(x, i, rows)
        for j in range(bins // 128):
            k = 8 * (i * (bins // 128) + j)
            at = (slice(8 * i, 8 * i + 8), slice(128 * j, 128 * (j + 1)))
            new[at] = old[at] * (total[k : k + 8, :] + more[k : k + 8, :]) * scale


def call(kernel, ins, outs, scratch=(), in_specs=(), out_specs=(), aliases=None, mib=28, flops=0):
    return pl.pallas_call(
        kernel,
        in_specs=list(in_specs) + [WHOLE] * (len(ins) - len(in_specs)),
        out_specs=list(out_specs) + [WHOLE] * (len(outs) - len(out_specs)),
        out_shape=[jax.ShapeDtypeStruct(*o) for o in outs],
        scratch_shapes=[pltpu.VMEM(*s) if isinstance(s, tuple) else s for s in scratch],
        input_output_aliases=aliases or {},
        compiler_params=pltpu.CompilerParams(vmem_limit_bytes=mib * 2**20),
        cost_estimate=pl.CostEstimate(flops=flops, bytes_accessed=0, transcendentals=0) if flops else None,
    )(*ins)


def hop(x, step):
    return lax.ppermute(x, "frames", [(i, i ^ step) for i in range(8)])


def body(spectrum, atoms_by_bin, activations, *, n_dev):
    swap = lambda x: lax.ppermute(x, "bins", [(0, 1), (1, 0)])
    bins, frames = spectrum.shape
    half = activations.shape[0]
    atoms = 2 * half
    rows = atoms_by_bin.shape[0]
    cube = n_dev == 8 and rows % 16 == 0
    size = frames // PIECES

    def basis_outs(k):
        return [((2 * k, bins), bf16), ((bins, 2 * k), bf16), ((k, 128), f32)]

    ordered = [((atoms, frames), f32), ((2 * atoms, frames), bf16)]
    h, h2, kept = call(
        functools.partial(own_kernel, cube=cube),
        [activations, atoms_by_bin],
        ordered + [((rows, bins), f32)],
        mib=16,
        flops=10**10,
    )
    raw = []
    if cube:
        near = [hop(atoms_by_bin, s) for s in (1, 2, 3)]
        far = hop(atoms_by_bin, GATHER_CROSS)
        raw = [far] + [hop(far, s) for s in (1, 2, 3)]
        near = [kept, *near]
    else:
        near = [lax.all_gather(atoms_by_bin, "frames", axis=0, tiled=True)]
    h, h2 = call(
        functools.partial(other_kernel, cube=cube),
        [swap(activations), h, h2],
        ordered,
        aliases={1: 0, 2: 1},
        mib=16,
        flops=10**9,
    )
    k = sum(w.shape[0] for w in near)
    w2, wt, mass = call(prepare_kernel, near, basis_outs(k), mib=16, flops=10**10)
    model = call(near_kernel, [wt, h2], [((bins, frames), f32)], mib=16, flops=10**9) if cube else []
    w2, wt, mass = [w2], [wt], [mass]
    numers = []
    for p in range(PIECES):
        numer, *made = call(
            functools.partial(first_kernel, start=p * size, n_parts=len(wt), masses=len(mass), raw=len(raw), near=cube),
            [spectrum, h2, *model, *w2, *wt, *mass, *raw],
            [((atoms + 8 * (p == 0), size), f32)] + (basis_outs(atoms - k) if raw else []),
            scratch=[((bins, size), bf16), ((bins, size), bf16)],
        )
        if raw:
            w2.append(made[0])
            wt.append(made[1])
        raw, mass = [], []
        numers.append((numer, swap(numer)))
    n_out = 4 if cube else 1
    block = ((rows * bins // 128 + 8, 128) if cube else (half, bins + 128), f32)
    carried = []
    for p in range(PIECES):
        final = p == PIECES - 1
        ins = [spectrum, h, *numers[0], *numers[p], *wt, *carried]
        outs = [
            ((half, frames), f32),
            ((half if final else atoms, bins), f32),
            ((atoms, 128), f32),
            ((bins, size), bf16),
            ((2 * atoms, size), bf16),
        ]
        fresh, *made = call(
            functools.partial(second_kernel, start=p * size, n_parts=len(wt), before=p > 0, n_out=n_out * final),
            ins + ([fresh] if p else []),
            outs + [block] * n_out * final,
            scratch=[
                ((atoms, size), f32),
                ((bins, size), bf16),
                ((atoms, 128), f32),
                ((half, bins), f32),
                pltpu.SemaphoreType.DMA((size // NC,)),
            ],
            in_specs=[WHOLE] * len(ins) + [HBM] if p else [],
            out_specs=[HBM],
            aliases={len(ins): 0} if p else None,
        )
        before, carried = carried[2:], made[:4]
    away = made[4:]
    home = call(third_kernel, carried + before, [block] * n_out, scratch=[((half, bins), f32)], flops=10**9)
    if cube:
        total = away[REDUCE_CROSS & 3]
        for s in (2, 1, 3):
            total = total + hop(away[s ^ (REDUCE_CROSS & 3)], s)
        more = hop(total, REDUCE_CROSS)
        total = home[0]
        for s in (1, 3, 2):
            total = total + hop(home[s], s)
        (new,) = call(last_kernel, [kept, total, more], [((rows, bins), f32)], mib=16)
        return fresh, new
    total = lax.psum_scatter(jnp.concatenate([*home, *away]), "frames", scatter_dimension=0, tiled=True)
    return fresh, atoms_by_bin * total[:, :bins] / total[:, bins : bins + 1]


def solution(mesh):
    return jax.shard_map(
        functools.partial(body, n_dev=mesh.shape["frames"]),
        mesh=mesh,
        in_specs=(P("bins", ("groups", "frames")), P("frames", ("groups", "bins")), P("bins", ("groups", "frames"))),
        out_specs=(P("bins", ("groups", "frames")), P("frames", ("groups", "bins"))),
        check_vma=False,
    )
```
